128 devices in a mesh: lon: 32 (over y, x_hi, z), lat: 4 (over x_lo, core).
Axes of the slice: x: 4 (x_hi: 2, x_lo: 2; x = x_hi * 2 + x_lo), y: 4, z: 4, core: 2. Of those that a mesh axis runs over, the one named last changes fastest.
Arguments:
- tracers: float32 [2, 10, 256, 16384], P(None, None, 'lat', 'lon'), may hold values from -6 to 6
- diffusivity: float32 [3, 10, 256, 16384], P(None, None, 'lat', 'lon'), may hold values from 0.02 to 0.12
- velocity: float32 [2, 10, 256, 16384], P(None, None, 'lat', 'lon'), may hold values from -0.16 to 0.16
- wet_mask: int32 [10, 256, 16384], P(None, 'lat', 'lon'), may hold values 0 or 1
- argo_rows: float32 [16384, 128], P(('lon', 'lat')), may hold values from -6 to 6
- argo_dest: int32 [16384, 1], P(('lon', 'lat')), may hold values from 0 to 127; in each aligned block of 128 rows (0 to 127, 128 to 255, ...) at most 2 rows name the same one
- argo_cols: int32 [16384], P(('lon', 'lat')), may hold values from 0 to 32767
- argo_count: int32 [128], P(('lon', 'lat')), may hold values from 96 to 128
- float_values: float32 [2048, 2, 128], P(('lon', 'lat')), may hold values from -6 to 6
- float_pos: float32 [2048, 2, 128], P(('lon', 'lat')), may hold values from 0 to 0.999
- float_dest: int32 [2048, 1], P(('lon', 'lat')), may hold values from 0 to 4; in each aligned block of 16 rows (0 to 15, 16 to 31, ...) at most 4 rows name the same one
Outputs:
- fields: float32 [2, 10, 256, 16384], P(None, None, 'lat', 'lon')
- floats_out: float32 [2560, 2, 128], P(('lon', 'lat'))
The draws below stay inside these ranges and needn't reach their ends.
Inputs may be any that keep to these rules, and one draw needn't show every extreme that they name: `argo_dest`: in the rows of one tile no tile is named more than 2 times, a bound that some block reaches. `float_dest`: in the rows of one tile no direction is named more than 4 times, a bound that some block reaches.
All inputs are finite; a program needn't handle non-finite values. No bound on the sum of `wet_mask` on one device may be relied on, other than what follows from the above.
Results may differ from the reference program's by a relative error of at most 0.0003.
Values sent between devices are 32-bit elements; how exact they have to be, the bound alone decides.
A program may use at most 128 MiB of HBM per device.

```python
import math
import jax
import jax.numpy as jnp
import numpy as np
from jax import lax

CX = 512
CY = 64
LEVELS = 10
STEPS = 3
PROF = 128
DEPTHS = 64
TILES = 128
ARGO_DEV = 128
ARGO_CAP = 2
FLOAT_BLK = 16
SLOTS = 4
RECORDS = 128
NX = 16384
NY = 256
N_LON = 32
N_LAT = 4


def set_ends(values, own_key, least, high):
    dims = values.shape
    index_at = [jax.random.randint(jax.random.fold_in(own_key, axis), (), 0, dims[axis]) for axis in range(len(dims))]
    values = values.at[tuple(index_at)].set(least)
    longest = dims.index(max(dims))
    index_at[longest] = (index_at[longest] + 1) % dims[longest]
    return values.at[tuple(index_at)].set(high)


def steps_of(key, dims, shards, smallest, top_value):
    def one(axis_at, shards_of):
        draws = jax.random.uniform(jax.random.fold_in(jax.random.fold_in(key, 6), axis_at), (shards_of,), jnp.float32, smallest / len(shards), top_value / len(shards))
        return jnp.repeat(jnp.exp(draws), dims[axis_at] // shards_of).reshape((-1,) + (1,) * (len(dims) - axis_at - 1))

    gain = one(*shards[0])
    for cut in shards[1:]:
        gain = gain * one(*cut)
    return gain


def routed_block(stream_key, own, number, rows, amount, top, bound, skew):
    ranking = jax.random.permutation(stream_key, amount)
    packed, ordinary = portions_of(amount, rows * top, bound, skew, True), portions_of(amount, rows * top, bound, skew, False)
    places = jnp.arange(amount)

    def named(lengths, turn):
        used = int((lengths > 0).sum())
        fixed = max(1, used // 4)
        passed = fixed + (places - fixed + turn * (used - fixed)) % max(1, amount - fixed)
        return jnp.zeros((amount,), jnp.int32).at[ranking[jnp.where(places < fixed, places, passed)]].set(jnp.asarray(lengths, jnp.int32))

    lengths = jnp.where(number % 4 == 0, named(packed, number // 4), named(ordinary, number - number // 4 - 1))
    mixed = jax.random.permutation(jax.random.fold_in(own, 3), amount)
    source_of, receiver = mixed[0:amount // 2 * 2:2], mixed[1:amount // 2 * 2:2]
    slack = jnp.minimum(lengths[source_of] - 1, bound - lengths[receiver]) // 2
    slack = jnp.where((source_of == ranking[0]) | (receiver == ranking[0]) | (lengths[receiver] == 0), 0, jnp.maximum(slack, 0))
    passed = jax.random.randint(jax.random.fold_in(own, 4), (amount // 2,), 0, 1 << 20) % (slack + 1)
    lengths = lengths.at[source_of].add(-passed).at[receiver].add(passed)
    items = jnp.searchsorted(jnp.cumsum(lengths), jnp.arange(rows * top), side="right").astype(jnp.int32)
    grid = items.reshape(top, rows).T
    grid = grid[jax.random.permutation(jax.random.fold_in(own, 1), rows)]
    turn = jax.random.randint(jax.random.fold_in(own, 2), (rows, 1), 0, top)
    return jnp.take_along_axis(grid, (jnp.arange(top)[None, :] + turn) % top, axis=1)


def portions_of(amount, total, limit, lean, full):
    weights = [(1 << 20) // math.isqrt(rank ** lean) + 1 for rank in range(1, amount + 1)]
    largest = limit if full else min(limit, max(-(-total // amount), total * weights[0] // sum(weights)))
    least = 1 if total - largest >= amount - 1 else 0
    holding, surplus = [largest] + [least] * (amount - 1), total - largest - least * (amount - 1)
    while surplus > 0:
        free = [i for i in range(1, amount) if holding[i] < largest] or [i for i in range(1, amount) if holding[i] < limit]
        whole, remaining = sum([weights[i] for i in free]), surplus
        for i in free:
            addition = min(limit - holding[i], max(1, remaining * weights[i] // whole), surplus)
            holding[i] = holding[i] + addition
            surplus = surplus - addition
    return np.array(holding)


def noise(stream_key, shape, deviation, limit, cuts=(), kind=jnp.bfloat16):
    level = steps_of(stream_key, shape, cuts, -0.22, 0.18) if cuts else 1.0
    values = jax.random.normal(stream_key, shape, jnp.float32) * deviation * level
    return jnp.minimum(jnp.maximum(values, -limit), limit).astype(kind)


def setup_inputs(seed: int = 0) -> dict:
    splits = jax.random.split(jax.random.key(seed), 12)
    tracers = noise(splits[0], (2, LEVELS, NY, NX), 1.0, 6.0, ((2, 4), (3, 32)), jnp.float32)
    diffusivity = jnp.clip(jnp.exp(math.log(0.12) - 1.7917595 * jax.random.uniform(splits[1], (3, LEVELS, NY, NX), jnp.float32) ** steps_of(splits[1], (3, LEVELS, NY, NX), ((2, 4), (3, 32)), -0.2, 0.2)), 0.02, 0.12)
    velocity = noise(splits[2], (2, LEVELS, NY, NX), 0.04, 0.16, ((2, 4), (3, 32)), jnp.float32)
    wet_mask = set_ends((jax.random.randint(splits[3], (LEVELS, NY, NX), 0, 10) < 9).astype(jnp.int32), jax.random.fold_in(splits[3], 1), 0, 1)
    argo_rows = noise(splits[4], (TILES * ARGO_DEV, PROF), 1.0, 6.0, ((0, 128),), jnp.float32)
    argo_dest_keys = jax.random.split(jax.random.fold_in(splits[5], 1), (TILES * ARGO_DEV) // ARGO_DEV)
    argo_dest_turns = jax.random.permutation(jax.random.fold_in(splits[5], 3), (TILES * ARGO_DEV) // ARGO_DEV)
    argo_dest = jax.vmap(lambda own, number: routed_block(jax.random.fold_in(splits[5], 2), own, number, ARGO_DEV, TILES, 1, ARGO_CAP, 2))(argo_dest_keys, argo_dest_turns).reshape((TILES * ARGO_DEV, 1))
    argo_cols = set_ends(jax.random.randint(splits[6], (TILES * ARGO_DEV,), 0, CY * CX), jax.random.fold_in(splits[6], 1), 0, (CY * CX) - 1).astype(jnp.int32)
    argo_count = set_ends(jax.random.randint(splits[7], (TILES,), ARGO_DEV * 3 // 4, ARGO_DEV + 1), jax.random.fold_in(splits[7], 1), ARGO_DEV * 3 // 4, ARGO_DEV).astype(jnp.int32)
    float_values = noise(splits[8], (TILES * FLOAT_BLK, 2, RECORDS), 1.0, 6.0, ((0, 128),), jnp.float32)
    float_pos = jnp.clip(0.999 * jax.random.uniform(splits[9], (TILES * FLOAT_BLK, 2, RECORDS), jnp.float32) ** steps_of(splits[9], (TILES * FLOAT_BLK, 2, RECORDS), ((0, 128),), -0.2, 0.2), 0.0, 0.999)
    float_dest_keys = jax.random.split(jax.random.fold_in(splits[10], 1), (TILES * FLOAT_BLK) // FLOAT_BLK)
    float_dest_turns = jax.random.permutation(jax.random.fold_in(splits[10], 3), (TILES * FLOAT_BLK) // FLOAT_BLK)
    float_dest = jax.vmap(lambda own, number: routed_block(jax.random.fold_in(splits[10], 2), own, number, FLOAT_BLK, 5, 1, SLOTS, 1))(float_dest_keys, float_dest_turns).reshape((TILES * FLOAT_BLK, 1))
    return {"tracers": tracers, "diffusivity": diffusivity, "velocity": velocity, "wet_mask": wet_mask, "argo_rows": argo_rows, "argo_dest": argo_dest, "argo_cols": argo_cols, "argo_count": argo_count, "float_values": float_values, "float_pos": float_pos, "float_dest": float_dest}


nudge_gain = 0.5


def tracer_step(padded, coeffs):
    diff_east = coeffs[0]
    diff_north = coeffs[1]
    diff_vert = coeffs[2]
    flow_east = coeffs[3]
    flow_north = coeffs[4]
    wet_cells = coeffs[5]
    left_cells = padded[:, :, 1:-1, :-1]
    right_cells = padded[:, :, 1:-1, 1:]
    open_east = wet_cells[:, 1:-1, :-1] * wet_cells[:, 1:-1, 1:]
    flux_east = open_east * (diff_east[:, 1:-1, :-1] * (right_cells - left_cells) - flow_east[:, 1:-1, :-1] * 0.5 * (left_cells + right_cells))
    lower_cells = padded[:, :, :-1, 1:-1]
    upper_cells = padded[:, :, 1:, 1:-1]
    open_north = wet_cells[:, :-1, 1:-1] * wet_cells[:, 1:, 1:-1]
    flux_north = open_north * (diff_north[:, :-1, 1:-1] * (upper_cells - lower_cells) - flow_north[:, :-1, 1:-1] * 0.5 * (lower_cells + upper_cells))
    inner = padded[:, :, 1:-1, 1:-1]
    wet_inner = wet_cells[:, 1:-1, 1:-1]
    vert_inner = diff_vert[:, 1:-1, 1:-1]
    flux_vert = wet_inner[:-1] * wet_inner[1:] * vert_inner[:-1] * (inner[:, 1:] - inner[:, :-1])
    zero_layer = jnp.zeros_like(inner[:, :1])
    vertical = jnp.concatenate([flux_vert, zero_layer], axis=1) - jnp.concatenate([zero_layer, flux_vert], axis=1)
    return inner + (flux_east[..., 1:] - flux_east[..., :-1]) + (flux_north[:, :, 1:] - flux_north[:, :, :-1]) + vertical


def interp_table(levels, depths):
    depth_pos = jnp.arange(depths, dtype=jnp.float32) * ((levels - 1) / (depths - 1))
    level_pos = jnp.arange(levels, dtype=jnp.float32)
    weights = jnp.maximum(0.0, 1.0 - jnp.abs(depth_pos[None, :] - level_pos[:, None]))
    return weights / jnp.sum(weights, axis=1, keepdims=True)


def pack_blocks(payload, target, groups, slots, fill):
    hits = (target[:, None] == jnp.arange(groups, dtype=jnp.int32)[None, :]).astype(jnp.int32)
    ranks = jnp.sum((jnp.cumsum(hits, axis=0) - hits) * hits, axis=1)
    empty = jnp.full((groups, slots) + payload.shape[1:], fill, payload.dtype)
    return empty.at[target, ranks].set(payload, mode="drop")


def sample_plane(plane, blocks, width, height):
    xpos = blocks[:, :, 2] * (width - 1)
    ypos = blocks[:, :, 3] * (height - 1)
    col_low = jnp.clip(jnp.floor(xpos).astype(jnp.int32), 0, width - 2)
    row_low = jnp.clip(jnp.floor(ypos).astype(jnp.int32), 0, height - 2)
    frac_x = xpos - col_low.astype(xpos.dtype)
    frac_y = ypos - row_low.astype(ypos.dtype)
    sample = ((1.0 - frac_y) * (1.0 - frac_x) * plane[:, row_low, col_low]
              + (1.0 - frac_y) * frac_x * plane[:, row_low, col_low + 1]
              + frac_y * (1.0 - frac_x) * plane[:, row_low + 1, col_low]
              + frac_y * frac_x * plane[:, row_low + 1, col_low + 1])
    updated = 0.5 * blocks[:, :, :2] + 0.5 * jnp.moveaxis(sample, 0, 2)
    return updated * blocks[:, :, 4:5]


def pad_grid(array):
    wrapped = jnp.pad(array, ((0, 0), (0, 0), (0, 0), (1, 1)), mode="wrap")
    return jnp.pad(wrapped, ((0, 0), (0, 0), (1, 1), (0, 0)))


def reference(tracers, diffusivity, velocity, wet_mask, argo_rows, argo_dest, argo_cols, argo_count, float_values, float_pos, float_dest):
    tile_count = N_LON * N_LAT
    total_rows = tile_count * ARGO_DEV
    row_ids = jnp.arange(total_rows, dtype=jnp.int32)
    source = row_ids // ARGO_DEV
    live = ((row_ids % ARGO_DEV) < argo_count[source]).astype(jnp.float32)
    target = argo_dest[:, 0]
    ycell = (target % N_LAT) * CY + argo_cols // CX
    xcell = (target // N_LAT) * CX + argo_cols % CX
    table = interp_table(LEVELS, DEPTHS)
    obs_temp = jnp.dot(argo_rows[:, :DEPTHS], table.T, precision=lax.Precision.HIGHEST)
    obs_salt = jnp.dot(argo_rows[:, DEPTHS:], table.T, precision=lax.Precision.HIGHEST)
    observed = jnp.stack([obs_temp.T, obs_salt.T])
    current = tracers[:, :, ycell, xcell]
    fields = tracers.at[:, :, ycell, xcell].add(nudge_gain * live * (observed - current))
    coeffs = jnp.concatenate([diffusivity, velocity, wet_mask[None].astype(jnp.float32)], axis=0)
    padded_c = pad_grid(coeffs)
    for number in range(STEPS):
        fields = tracer_step(pad_grid(fields), padded_c)
    planes = fields[:, 0].reshape(2, N_LAT, CY, N_LON, CX).transpose(3, 1, 0, 2, 4)
    blocks = jnp.concatenate([float_values, float_pos, jnp.ones_like(float_pos[:, :1])], axis=1)
    blocks = blocks.reshape(N_LON, N_LAT, FLOAT_BLK, 5, RECORDS)
    route = float_dest[:, 0].reshape(N_LON, N_LAT, FLOAT_BLK)
    packer = jax.vmap(jax.vmap(lambda payload, aims: pack_blocks(payload, aims, 5, SLOTS, 0.0)))
    buffers = packer(blocks, route)
    empty_row = jnp.zeros_like(buffers[:, :1, 3])
    group_one = jnp.roll(buffers[:, :, 1], 1, axis=0)
    group_two = jnp.roll(buffers[:, :, 2], -1, axis=0)
    group_three = jnp.concatenate([empty_row, buffers[:, :-1, 3]], axis=1)
    group_four = jnp.concatenate([buffers[:, 1:, 4], empty_row], axis=1)
    arrived = jnp.stack([buffers[:, :, 0], group_one, group_two, group_three, group_four], axis=2)
    sampler = jax.vmap(jax.vmap(lambda plane, blk: sample_plane(plane, blk, CX, CY)))
    result = sampler(planes, arrived)
    return fields, result.reshape(tile_count * 5 * SLOTS, 2, RECORDS)
```

```python
import functools

import jax
import jax.numpy as jnp
from jax import lax
from jax.experimental import pallas as pl
from jax.experimental.pallas import tpu as pltpu
from jax.sharding import PartitionSpec as P

MESH = pl.DeviceIdType.MESH
F32, BF16, I32 = jnp.float32, jnp.bfloat16, jnp.int32

LEVELS, H, W = 10, 64, 512
EH, EW = 72, 640
STRIPS = EH // 8
PAY = 21


def split(x):
    high = x.astype(BF16)
    return high, (x - high.astype(F32)).astype(BF16)


def iota(shape, dim):
    return lax.broadcasted_iota(I32, shape, dim)


def column_of(row):
    n = row.shape[1]
    wide = jnp.broadcast_to(row, (n, n))
    return jnp.sum(jnp.where(iota((n, n), 0) == iota((n, n), 1), wide, 0.0), axis=1, keepdims=True)


def ranks_of(row):
    n = row.shape[1]
    earlier = (column_of(row) == row) & (iota((n, n), 0) < iota((n, n), 1))
    return jnp.sum(earlier.astype(F32), axis=0, keepdims=True)


def places():
    lon, lat = lax.axis_index("lon"), lax.axis_index("lat")
    z, b = lon % 4, lon // 4
    u, v = (b % 2) * 4 + lat, (b // 2) * 4 + z
    return lon, lat, u, v


def device_of(u, v):
    return ((v // 4) * 8 + (u // 4) * 4 + v % 4, u % 4)


def kernel(
    tr_hbm, di_hbm, ve_hbm, wet_hbm, rows_ref, dest_ref, cols_ref, count_ref, fval_ref, fpos_ref, fdest_ref,
    out_ref, fout_ref,
    c0, c1, dx, vx, wi, wf, vbuf, packs, from_w, from_e, from_nw, from_sw, from_ne, from_se,
    msg, mid, got, fsend, fgot, amat, hot,
    load_sem, p1_s, p1_r, p2_s, p2_r, ns_s, ns_r, ew_s, ew_r, fl_s, fl_r,
):
    lon, lat, u, v = places()
    east, west = ((lon + 1) % 32, lat), ((lon + 31) % 32, lat)
    north, south = (lon, (lat + 1) % 4), (lon, (lat + 3) % 4)
    ne, se = (east[0], north[1]), (east[0], south[1])
    nw, sw = (west[0], north[1]), (west[0], south[1])
    barrier = pltpu.get_barrier_semaphore()

    @pl.loop(1, 8)
    def _(d):
        pl.semaphore_signal(barrier, inc=1, device_id=device_of((u + d) % 8, v), device_id_type=MESH)

    @pl.loop(1, 16)
    def _(d):
        pl.semaphore_signal(barrier, inc=1, device_id=device_of(u, (v + d) % 16), device_id_type=MESH)

    for peer in (east, west, north, south, ne, se, nw, sw):
        pl.semaphore_signal(barrier, inc=1, device_id=peer, device_id_type=MESH)

    loads = [
        pltpu.make_async_copy(di_hbm, dx.at[:, :, pl.ds(0, H), pl.ds(0, W)], load_sem.at[0]),
        pltpu.make_async_copy(ve_hbm, vx.at[:, :, pl.ds(0, H), pl.ds(0, W)], load_sem.at[1]),
        pltpu.make_async_copy(wet_hbm, wi.at[:, pl.ds(0, H)], load_sem.at[2]),
        pltpu.make_async_copy(tr_hbm, c0.at[:, pl.ds(0, LEVELS), pl.ds(0, H), pl.ds(0, W)], load_sem.at[3]),
    ]
    for copy in loads:
        copy.start()

    lane = iota((128, 128), 1)
    sub = iota((128, 128), 0)
    level = jnp.where(sub >= PAY, sub - PAY, sub)
    tracer = jnp.where(level >= LEVELS, 1, 0)
    level = level - tracer * LEVELS
    depth = lane - tracer * 64
    weight = jnp.maximum(0.0, 1.0 - jnp.abs(depth.astype(F32) * ((LEVELS - 1) / 63.0) - level.astype(F32)))
    weight = jnp.where((depth >= 0) & (depth < 64), weight, 0.0)
    total = jnp.sum(weight, axis=1, keepdims=True)
    table = 0.5 * weight / jnp.where(total > 0.0, total, 1.0)
    pay = lax.dot_general(
        table, rows_ref[...], (((1,), (1,)), ((), ())), precision=lax.Precision.HIGHEST, preferred_element_type=F32
    )
    cell = (cols_ref[...] + 1).astype(F32)
    pay = jnp.where((sub == PAY - 1) | (sub == 2 * PAY - 1), jnp.broadcast_to(cell, (128, 128)), pay)
    pay = jnp.concatenate([jnp.where(sub < PAY, pay, 0.0), jnp.where((sub >= PAY) & (sub < 2 * PAY), pay, 0.0)], axis=1)
    live = iota((1, 128), 1) < count_ref[0]
    dest = jnp.where(live, dest_ref[...], -5).astype(F32)
    rank = ranks_of(dest)
    tile = ((sub % 32) * 4 + sub // 32).astype(F32)
    first = jnp.where((tile == dest) & (rank == 0.0), 1.0, 0.0)
    second = jnp.where((tile == dest) & (rank == 1.0), 1.0, 0.0)
    chosen = jnp.concatenate([first, second], axis=1).astype(BF16)
    ordered = sum(
        lax.dot_general(chosen, part, (((1,), (1,)), ((), ())), preferred_element_type=F32) for part in split(pay)
    )
    for b in range(4):
        full = pltpu.roll(ordered[32 * b : 32 * b + 32], 2 * PAY, 1)
        if b > 0:
            full = full + ordered[32 * b - 32 : 32 * b]
        if b < 3:
            full = full + pltpu.roll(ordered[32 * b + 32 : 32 * b + 64], 4 * PAY, 1)
        for h in range(2):
            for y in range(4):
                for s in range(6):
                    at = (8 * y + 4 * h + s - 1) % 32
                    msg[4 * h + b, y, s] = full[at : at + 1]

    fdest = fdest_ref[...].astype(F32)
    place = 8.0 * fdest + ranks_of(fdest)
    fhot = (iota((40, 16), 0).astype(F32) == place).astype(F32)
    fpay = jnp.concatenate([fval_ref[:, 0], fval_ref[:, 1], fpos_ref[:, 0], fpos_ref[:, 1]], axis=1)
    fordered = jnp.dot(fhot, fpay, precision=lax.Precision.HIGHEST, preferred_element_type=F32)
    fsend[:, :, pl.ds(0, 512)] = fordered.reshape(5, 8, 512)
    flags = jnp.broadcast_to(jnp.sum(fhot, axis=1, keepdims=True), (40, 128))
    fsend[:, :, pl.ds(512, 128)] = flags.reshape(5, 8, 128)

    pl.semaphore_wait(barrier, 30)

    def remote(src, dst, s, r, peer):
        return pltpu.make_async_remote_copy(
            src_ref=src, dst_ref=dst, send_sem=s, recv_sem=r, device_id=peer, device_id_type=MESH
        )

    @pl.loop(1, 8)
    def _(d):
        t = (u + d) % 8
        remote(msg.at[t], mid.at[d], p1_s, p1_r, device_of(t, v)).start()

    top, bottom = pl.ds(61, 3), pl.ds(0, 3)
    low, high = pl.ds(69, 3), pl.ds(64, 3)
    wide = pl.ds(0, W)
    edge = []
    for i, (src, dst) in enumerate(((di_hbm, dx), (ve_hbm, vx), (tr_hbm, c0))):
        edge.append(remote(src.at[:, :, top], dst.at[:, pl.ds(0, LEVELS), low, wide], ns_s.at[i], ns_r.at[i], north))
        edge.append(remote(src.at[:, :, bottom], dst.at[:, pl.ds(0, LEVELS), high, wide], ns_s.at[4 + i], ns_r.at[4 + i], south))
    edge.append(remote(wet_hbm.at[:, top], wi.at[:, low], ns_s.at[3], ns_r.at[3], north))
    edge.append(remote(wet_hbm.at[:, bottom], wi.at[:, high], ns_s.at[7], ns_r.at[7], south))
    for i, peer in enumerate((east, west, north, south)):
        edge.append(remote(fsend.at[1 + i], fgot.at[i], fl_s.at[i], fl_r.at[i], peer))
    for copy in edge:
        copy.start()
    mid[0] = msg[u]

    for copy in loads:
        copy.wait()

    lane64 = iota((H, 128), 1)

    def planes_of(t):
        for q in range(20):
            n, k = q // LEVELS, q % LEVELS
            yield q, ((c0, (n, k)), (dx, (0, k)) if n == 0 else (vx, (0, k)), (dx, (1, k)) if n == 0 else (vx, (1, k)), (dx, (2, k)) if n == 0 else (wf, (k,)))[t]

    for k in range(LEVELS):
        wf[k, pl.ds(0, H), wide] = wi[k, pl.ds(0, H)].astype(F32)
    for t in range(4):
        acc = jnp.zeros((H, 128), F32)
        for q, (ref, at) in planes_of(t):
            left = ref[at + (pl.ds(0, H), pl.ds(0, 128))]
            right = ref[at + (pl.ds(0, H), pl.ds(384, 128))]
            both = pltpu.roll(jnp.where(lane64 < 3, left, right), 6 * q + 3, 1)
            acc = jnp.where(lane64 >= 6 * q, both, acc)
        packs[t] = acc
    sides = [
        remote(packs, from_w, ew_s.at[0], ew_r.at[0], east),
        remote(packs, from_e, ew_s.at[1], ew_r.at[1], west),
        remote(packs.at[:, pl.ds(56, 8)], from_sw, ew_s.at[2], ew_r.at[2], ne),
        remote(packs.at[:, pl.ds(56, 8)], from_se, ew_s.at[3], ew_r.at[3], nw),
        remote(packs.at[:, pl.ds(0, 8)], from_nw, ew_s.at[4], ew_r.at[4], se),
        remote(packs.at[:, pl.ds(0, 8)], from_ne, ew_s.at[5], ew_r.at[5], sw),
    ]
    for copy in sides:
        copy.start()

    done = remote(mid.at[pl.ds(1, 7)], mid.at[pl.ds(1, 7)], p1_s, p1_r, east)
    done.wait_send()
    done.wait_recv()

    @pl.loop(1, 16)
    def _(d):
        t = (v + d) % 16
        remote(mid.at[:, t // 4, pl.ds(t % 4, 3)], got.at[d], p2_s, p2_r, device_of(u, t)).start()

    got[0] = mid[:, v // 4, pl.ds(v % 4, 3)]

    sub8 = iota((8, EW), 0)

    def up(cur, nxt):
        n = cur.shape[1]
        return jnp.where(sub8[:, :n] == 7, pltpu.roll(nxt, 7, 0), pltpu.roll(cur, 7, 0))

    def coefficients(k, strip, a, b):
        rows = pl.ds(8 * strip, 8)
        after = pl.ds(8 * ((strip + 1) % STRIPS), 8)
        lanes = pl.ds(a, b - a)
        w = wf[k, rows, lanes]
        if b < EW:
            w_e = pltpu.roll(wf[k, rows, pl.ds(a, b - a + 128)], b - a + 127, 1)[:, : b - a]
        elif a == 0:
            w_e = pltpu.roll(w, EW - 1, 1)
        else:
            w_e = jnp.concatenate([w, wf[k, rows, pl.ds(0, 128)]], axis=1)
            w_e = pltpu.roll(w_e, b - a + 127, 1)[:, : b - a]
        w_n = up(w, wf[k, after, lanes])
        w_v = wf[k + 1, rows, lanes]
        for i, other in ((0, w_e), (1, w_n)):
            d, f, open_ = dx[i, k, rows, lanes], 0.5 * vx[i, k, rows, lanes], w * other
            dx[i, k, rows, lanes] = open_ * (d - f)
            vx[i, k, rows, lanes] = open_ * (d + f)
        dx[2, k, rows, lanes] = w * w_v * dx[2, k, rows, lanes]

    wf[LEVELS] = jnp.zeros((EH, EW), F32)
    for n in range(2):
        c0[n, LEVELS] = jnp.zeros((EH, EW), F32)
        c1[n, LEVELS] = jnp.zeros((EH, EW), F32)

    @pl.loop(0, LEVELS)
    def _(k):
        for strip in range(7):
            coefficients(k, strip, 0, 384)

    for i in range(4):
        edge[8 + i].wait()
    blocks = [fsend[0]] + [fgot[i] for i in range(4)]
    reach = {3: jnp.where(lat > 0, 1.0, 0.0), 4: jnp.where(lat < 3, 1.0, 0.0)}
    cells = iota((W, 128), 0)
    lows, fracs = [], []
    for g in range(5):
        for s in range(4):
            xpos = blocks[g][s : s + 1, 256:384] * (W - 1.0)
            lowest = jnp.clip(jnp.floor(xpos).astype(I32), 0, W - 2)
            fracs.append(xpos - lowest.astype(F32))
            hot[:, pl.ds(512 * g + 128 * s, 128)] = jnp.where(cells == lowest, 1.0, 0.0).astype(BF16)

    for copy in edge[:8] + sides:
        copy.wait()
    inside = jnp.where(iota((8, W), 0) < 4, jnp.where(lat < 3, 1, 0), jnp.where(lat > 0, 1, 0))
    for k in range(LEVELS):
        wf[k, pl.ds(H, 8), wide] = jnp.where(inside > 0, wi[k, pl.ds(H, 8)].astype(F32), 0.0)
    lane8 = iota((8, 128), 1)
    side = []
    for t in range(4):
        body = jnp.where(lane64 % 6 < 3, from_w[t], from_e[t])
        upper = jnp.where(lane8 % 6 < 3, from_nw[t], from_ne[t])
        lower = jnp.where(lane8 % 6 < 3, from_sw[t], from_se[t])
        side.append(jnp.concatenate([body, jnp.where(sub8[:, :128] < 4, upper, lower)], axis=0))

    done = remote(got.at[pl.ds(1, 15)], got.at[pl.ds(1, 15)], p2_s, p2_r, east)
    done.wait_send()
    done.wait_recv()

    cols_of, rows_of, vals, valsT = {}, {}, {}, {}
    for g in range(3):
        vals[g] = got[:, :, g].reshape(128, 128)
        valsT[g] = vals[g].T
        cols_of[g] = (vals[g].astype(I32) - 1) & (W - 1)
        rows_of[g] = (valsT[g].astype(I32) - 1) >> 9

    def base(dlat, slot):
        return PAY * (2 * (dlat + 1) + slot)

    wide_lane = iota((128, W), 1)

    def column_hot(g, dlat):
        parts = []
        for slot in range(2):
            at = base(dlat, slot) + 20
            parts.append(jnp.where(wide_lane == cols_of[g][:, at : at + 1], 1.0, 0.0))
        return jnp.concatenate(parts, axis=0).astype(BF16)

    def row_ids(g, dlat):
        ats = [base(dlat, slot) + 20 for slot in range(2)]
        return jnp.concatenate([rows_of[g][at : at + 1] for at in ats], axis=1)

    def value_row(g, dlat, c):
        ats = [base(dlat, slot) + c for slot in range(2)]
        return jnp.concatenate([valsT[g][at : at + 1] for at in ats], axis=1)

    own = jnp.where(iota((H, 256), 0) == row_ids(1, 0), 1.0, 0.0)
    for c in range(20):
        value = value_row(1, 0, c)
        value_hi = value.astype(BF16).astype(F32)
        amat[pl.ds(H * c, H), pl.ds(0, 256)] = (own * value_hi).astype(BF16)
        amat[pl.ds(H * c, H), pl.ds(256, 256)] = (own * (value - value_hi)).astype(BF16)
    amat[pl.ds(H * 20, H), pl.ds(0, 256)] = own.astype(BF16)
    amat[pl.ds(H * 20, H), pl.ds(256, 256)] = jnp.zeros((H, 256), BF16)
    onto = column_hot(1, 0)
    onto = jnp.concatenate([onto, onto], axis=0)
    added = jnp.dot(amat[...], onto, preferred_element_type=F32)
    keep = 1.0 - 0.5 * added[H * 20 :]
    for c in range(20):
        at = (c // LEVELS, c % LEVELS, pl.ds(0, H), wide)
        c0[at] = c0[at] * keep + added[H * c : H * c + H]

    sub256 = iota((8, 256), 0)
    north_ids, south_ids = row_ids(1, 1), row_ids(1, -1)
    hits = [
        jnp.where((sub256 == north_ids) & (sub256 < 4), 1.0, 0.0),
        jnp.where((sub256 + 56 == south_ids) & (sub256 >= 4), 1.0, 0.0),
    ]
    hits = jnp.concatenate(hits, axis=1)
    parts = []
    for c in range(20):
        parts.append(hits * jnp.concatenate([value_row(1, 1, c), value_row(1, -1, c)], axis=1))
    parts.append(hits)
    parts.append(jnp.zeros_like(hits))
    near = jnp.concatenate(parts, axis=0)
    onto = jnp.concatenate([column_hot(1, 1), column_hot(1, -1)], axis=0)
    added = sum(jnp.dot(part, onto, preferred_element_type=F32) for part in split(near))
    keep = 1.0 - 0.5 * added[160:168]
    for c in range(20):
        at = (c // LEVELS, c % LEVELS, pl.ds(H, 8), wide)
        c0[at] = c0[at] * keep + added[8 * c : 8 * c + 8]

    spread_from, spread_to = iota((128, 6 * 128), 0), iota((128, 6 * 128), 1)
    spread_lane = spread_to % 128
    spread = (spread_from == PAY * (spread_to // 128) + spread_lane // 6) & (spread_lane < 120)
    spread = jnp.where(spread, 1.0, 0.0).astype(BF16)
    sub72 = iota((EH, 128), 0)
    lane128 = iota((128, 128), 1)
    within = lane128 % 6
    pick, hi_parts, lo_parts, ones = [], [], [], []
    for g in (0, 2):
        grown = [jnp.dot(part, spread, preferred_element_type=F32) for part in split(vals[g])]
        target = jnp.where(within < 3, 509 + within, -1) if g == 0 else jnp.where(within >= 3, within - 3, -1)
        target = jnp.where(lane128 < 120, target, -1)
        for dlat in (-1, 0, 1):
            for slot in range(2):
                at = base(dlat, slot) + 20
                ids = rows_of[g][at : at + 1]
                if dlat == 1:
                    ids = jnp.where((ids >= 0) & (ids < 4), ids + H, -1)
                elif dlat == -1:
                    ids = jnp.where(ids >= 60, ids + 8, -1)
                pick.append(jnp.where(sub72 == ids, 1.0, 0.0))
                match = jnp.where(cols_of[g][:, at : at + 1] == target, 1.0, 0.0)
                block = 2 * (dlat + 1) + slot
                hi_parts.append(match * grown[0][:, 128 * block : 128 * block + 128])
                lo_parts.append(match * grown[1][:, 128 * block : 128 * block + 128])
                ones.append(match)
    pick = jnp.concatenate(pick, axis=1).astype(BF16)
    onto = jnp.concatenate([jnp.concatenate(p, axis=0).astype(BF16) for p in (hi_parts, lo_parts, ones)], axis=1)
    added = jnp.dot(pick, onto, preferred_element_type=F32)
    side[0] = side[0] * (1.0 - 0.5 * added[:, 256:384]) + added[:, 0:128] + added[:, 128:256]

    for t in range(4):
        for q, (ref, at) in planes_of(t):
            values = pltpu.roll(side[t], (128 - 6 * q - 3) % 128, 1)
            if ref is wf:
                edge_rows = jnp.where(inside[:, :128] > 0, values[H:], 0.0)
                values = jnp.concatenate([values[:H], edge_rows], axis=0)
            ref[at + (slice(None), pl.ds(W, 128))] = values

    @pl.loop(0, LEVELS)
    def _(k):
        for strip in range(7):
            coefficients(k, strip, 384, EW)
        for strip in (7, 8):
            coefficients(k, strip, 0, EW)

    def step(src, dst, last):
        vbuf[...] = jnp.zeros((2, EH, EW), F32)

        @pl.loop(0, LEVELS)
        def _(k):
            def strip_of(n, i):
                return src[n, k, pl.ds(8 * (i % STRIPS), 8), :]

            def face_n(i, cur, cur_n):
                rows = pl.ds(8 * i, 8)
                return dx[1, k, rows, :] * cur_n - vx[1, k, rows, :] * cur

            cur, turned, below = {}, {}, {}
            for n in range(2):
                tail, head = strip_of(n, 8), strip_of(n, 0)
                turned[n] = pltpu.roll(head, 7, 0)
                tail_n = jnp.where(sub8 == 7, turned[n], pltpu.roll(tail, 7, 0))
                below[n] = pltpu.roll(face_n(8, tail, tail_n), 1, 0)
                cur[n] = head
            for i in range(8 if last else STRIPS):
                rows = pl.ds(8 * i, 8)
                for n in range(2):
                    here = cur[n]
                    after = strip_of(n, i + 1)
                    after_turned = pltpu.roll(after, 7, 0)
                    flux_n = face_n(i, here, jnp.where(sub8 == 7, after_turned, turned[n]))
                    flux_turned = pltpu.roll(flux_n, 1, 0)
                    new = here + (flux_n - jnp.where(sub8 == 0, below[n], flux_turned))
                    flux_e = dx[0, k, rows, :] * pltpu.roll(here, EW - 1, 1) - vx[0, k, rows, :] * here
                    new = new + (flux_e - pltpu.roll(flux_e, 1, 1))
                    flux_v = dx[2, k, rows, :] * (src[n, k + 1, rows, :] - here)
                    new = new + (flux_v - vbuf[n, rows, :])
                    vbuf[n, rows, :] = flux_v
                    if last:
                        dst[n, k, rows, :] = new[:, :W]
                    else:
                        dst[n, k, rows, :] = new
                    cur[n], turned[n], below[n] = after, after_turned, flux_turned

    step(c0, c1, False)
    step(c1, c0, False)
    step(c0, out_ref, True)

    plane = jnp.concatenate([out_ref[0, 0], out_ref[1, 0]], axis=0)
    nexts = pltpu.roll(plane, W - 1, 1)
    lhs = jnp.concatenate(list(split(plane)) + list(split(nexts)), axis=0)
    line = iota((H, 128), 0).astype(F32)
    for g in range(5):
        res = jnp.dot(lhs, hot[:, pl.ds(512 * g, 512)], preferred_element_type=F32)
        for s in range(4):
            part = res[:, 128 * s : 128 * s + 128]
            frac = fracs[4 * g + s]
            along = (1.0 - frac) * (part[0:128] + part[128:256]) + frac * (part[256:384] + part[384:512])
            ypos = blocks[g][s : s + 1, 384:512] * (H - 1.0)
            tent = jnp.maximum(0.0, 1.0 - jnp.abs(ypos - line))
            flag = blocks[g][s : s + 1, 512:640]
            for n in range(2):
                sample = jnp.sum(along[H * n : H * n + H] * tent, axis=0, keepdims=True)
                value = flag * (0.5 * blocks[g][s : s + 1, 128 * n : 128 * n + 128] + 0.5 * sample)
                if g in reach:
                    value = reach[g] * value
                fout_ref[4 * g + s, pl.ds(n, 1), :] = value


def shards(tracers, diffusivity, velocity, wet_mask, argo_rows, argo_dest, argo_cols, argo_count, float_values, float_pos, float_dest):
    vmem = pl.BlockSpec(memory_space=pltpu.VMEM)
    hbm = pl.BlockSpec(memory_space=pl.ANY)
    smem = pl.BlockSpec(memory_space=pltpu.SMEM)
    dma, scratch = pltpu.SemaphoreType.DMA, pltpu.VMEM
    return pl.pallas_call(
        kernel,
        out_shape=(
            jax.ShapeDtypeStruct(tracers.shape, F32),
            jax.ShapeDtypeStruct((20, 2, 128), F32),
        ),
        in_specs=[hbm] * 4 + [vmem, vmem, vmem, smem, vmem, vmem, vmem],
        out_specs=(vmem, vmem),
        scratch_shapes=[
            scratch((2, LEVELS + 1, EH, EW), F32),
            scratch((2, LEVELS + 1, EH, EW), F32),
            scratch((3, LEVELS, EH, EW), F32),
            scratch((2, LEVELS, EH, EW), F32),
            scratch((LEVELS, EH, W), I32),
            scratch((LEVELS + 1, EH, EW), F32),
            scratch((2, EH, EW), F32),
            scratch((4, H, 128), F32),
            scratch((4, H, 128), F32),
            scratch((4, H, 128), F32),
            scratch((4, 8, 128), F32),
            scratch((4, 8, 128), F32),
            scratch((4, 8, 128), F32),
            scratch((4, 8, 128), F32),
            scratch((8, 4, 6, 1, 128), F32),
            scratch((8, 4, 6, 1, 128), F32),
            scratch((16, 8, 3, 1, 128), F32),
            scratch((5, 8, 640), F32),
            scratch((4, 8, 640), F32),
            scratch((H * 21, 512), BF16),
            scratch((W, 2560), BF16),
            dma((4,)), dma, dma, dma, dma, dma((8,)), dma((8,)), dma((6,)), dma((6,)), dma((4,)), dma((4,)),
        ],
        compiler_params=pltpu.CompilerParams(
            collective_id=1, has_side_effects=True, vmem_limit_bytes=60 * 1024 * 1024
        ),
    )(
        tracers, diffusivity, velocity, wet_mask, argo_rows, argo_dest.reshape(1, -1), argo_cols.reshape(1, -1),
        argo_count, float_values, float_pos, float_dest.reshape(1, -1),
    )


def solution(mesh):
    grid4, grid3 = P(None, None, "lat", "lon"), P(None, "lat", "lon")
    tiles = ("lon", "lat")
    return jax.shard_map(
        shards,
        mesh=mesh,
        in_specs=(
            grid4, grid4, grid4, grid3, P(tiles, None), P(tiles, None), P(tiles), P(tiles),
            P(tiles, None, None), P(tiles, None, None), P(tiles, None),
        ),
        out_specs=(grid4, P(tiles, None, None)),
        check_vma=False,
    )
```

```python
import functools

import jax
import jax.numpy as jnp
from jax import lax
from jax.experimental import pallas as pl
from jax.experimental.pallas import tpu as pltpu
from jax.sharding import PartitionSpec as P

MESH = pl.DeviceIdType.MESH
F32, BF16, I32 = jnp.float32, jnp.bfloat16, jnp.int32

LEVELS, H, W = 10, 64, 512
EH, EW = 72, 640
STRIPS = EH // 8
GAP = 3
PAY = 21


def split(x):
    high = x.astype(BF16)
    return high, (x - high.astype(F32)).astype(BF16)


def iota(shape, dim):
    return lax.broadcasted_iota(I32, shape, dim)


def column_of(row):
    n = row.shape[1]
    wide = jnp.broadcast_to(row, (n, n))
    return jnp.sum(jnp.where(iota((n, n), 0) == iota((n, n), 1), wide, 0.0), axis=1, keepdims=True)


def ranks_of(row):
    n = row.shape[1]
    earlier = (column_of(row) == row) & (iota((n, n), 0) < iota((n, n), 1))
    return jnp.sum(earlier.astype(F32), axis=0, keepdims=True)


def places():
    lon, lat = lax.axis_index("lon"), lax.axis_index("lat")
    z, b = lon % 4, lon // 4
    u, v = (b % 2) * 4 + lat, (b // 2) * 4 + z
    return lon, lat, u, v


def device_of(u, v):
    return ((v // 4) * 8 + (u // 4) * 4 + v % 4, u % 4)


def kernel(
    tr_hbm, di_hbm, ve_hbm, wet_hbm, rows_ref, dest_ref, cols_ref, count_ref, fval_ref, fpos_ref, fdest_ref,
    out_ref, fout_ref,
    c0, c1, dx, vx, wi, wf, vbuf, packs, from_w, from_e, from_nw, from_sw, from_ne, from_se,
    msg, mid, got, fsend, fgot, amat, hot, spread,
    load_sem, p1_s, p1_r, p2_s, p2_r, ns_s, ns_r, ew_s, ew_r, fl_s, fl_r, row_s, row_r,
):
    lon, lat, u, v = places()
    east, west = ((lon + 1) % 32, lat), ((lon + 31) % 32, lat)
    north, south = (lon, (lat + 1) % 4), (lon, (lat + 3) % 4)
    ne, se = (east[0], north[1]), (east[0], south[1])
    nw, sw = (west[0], north[1]), (west[0], south[1])
    barrier = pltpu.get_barrier_semaphore()

    @pl.loop(1, 8)
    def _(d):
        pl.semaphore_signal(barrier, inc=1, device_id=device_of((u + d) % 8, v), device_id_type=MESH)

    @pl.loop(1, 16)
    def _(d):
        pl.semaphore_signal(barrier, inc=1, device_id=device_of(u, (v + d) % 16), device_id_type=MESH)

    for peer in (east, west, north, south, ne, se, nw, sw):
        pl.semaphore_signal(barrier, inc=1, device_id=peer, device_id_type=MESH)

    loads = [
        pltpu.make_async_copy(di_hbm, dx.at[:, :, pl.ds(0, H), pl.ds(0, W)], load_sem.at[0]),
        pltpu.make_async_copy(ve_hbm, vx.at[:, :, pl.ds(0, H), pl.ds(0, W)], load_sem.at[1]),
        pltpu.make_async_copy(wet_hbm, wi.at[:, pl.ds(0, H)], load_sem.at[2]),
        pltpu.make_async_copy(tr_hbm, c0.at[:, pl.ds(0, LEVELS), pl.ds(0, H), pl.ds(0, W)], load_sem.at[3]),
    ]
    for copy in loads:
        copy.start()

    lane = iota((128, 128), 1)
    sub = iota((128, 128), 0)
    level = jnp.where(sub >= PAY, sub - PAY, sub)
    tracer = jnp.where(level >= LEVELS, 1, 0)
    level = level - tracer * LEVELS
    depth = lane - tracer * 64
    weight = jnp.maximum(0.0, 1.0 - jnp.abs(depth.astype(F32) * ((LEVELS - 1) / 63.0) - level.astype(F32)))
    weight = jnp.where((depth >= 0) & (depth < 64), weight, 0.0)
    total = jnp.sum(weight, axis=1, keepdims=True)
    table = 0.5 * weight / jnp.where(total > 0.0, total, 1.0)
    pay = lax.dot_general(
        table, rows_ref[...], (((1,), (1,)), ((), ())), precision=lax.Precision.HIGHEST, preferred_element_type=F32
    )
    cell = (cols_ref[...] + 1).astype(F32)
    pay = jnp.where((sub == PAY - 1) | (sub == 2 * PAY - 1), jnp.broadcast_to(cell, (128, 128)), pay)
    pay = jnp.concatenate([jnp.where(sub < PAY, pay, 0.0), jnp.where((sub >= PAY) & (sub < 2 * PAY), pay, 0.0)], axis=1)
    live = iota((1, 128), 1) < count_ref[0]
    dest = jnp.where(live, dest_ref[...], -5).astype(F32)
    rank = ranks_of(dest)
    tile = ((sub % 32) * 4 + sub // 32).astype(F32)
    first = jnp.where((tile == dest) & (rank == 0.0), 1.0, 0.0)
    second = jnp.where((tile == dest) & (rank == 1.0), 1.0, 0.0)
    chosen = jnp.concatenate([first, second], axis=1).astype(BF16)
    ordered = sum(
        lax.dot_general(chosen, part, (((1,), (1,)), ((), ())), preferred_element_type=F32) for part in split(pay)
    )
    for b in range(4):
        mine = ordered[32 * b : 32 * b + 32]
        full = pltpu.roll(mine, 1, 0) + pltpu.roll(mine, 2 * PAY, 1) + pltpu.roll(pltpu.roll(mine, 31, 0), 4 * PAY, 1)
        for h in range(2):
            for y in range(4):
                for z in range(4):
                    at = 8 * y + 4 * h + z
                    msg[4 * h + b, y, z] = full[at : at + 1]

    fdest = fdest_ref[...].astype(F32)
    place = 8.0 * fdest + ranks_of(fdest)
    fhot = (iota((40, 16), 0).astype(F32) == place).astype(F32)
    fpay = jnp.concatenate([fval_ref[:, 0], fval_ref[:, 1], fpos_ref[:, 0], fpos_ref[:, 1]], axis=1)
    fordered = jnp.dot(fhot, fpay, precision=lax.Precision.HIGHEST, preferred_element_type=F32)
    fsend[:, :, pl.ds(0, 512)] = fordered.reshape(5, 8, 512)
    flags = jnp.broadcast_to(jnp.sum(fhot, axis=1, keepdims=True), (40, 128))
    fsend[:, :, pl.ds(512, 128)] = flags.reshape(5, 8, 128)

    pl.semaphore_wait(barrier, 30)

    def remote(src, dst, s, r, peer):
        return pltpu.make_async_remote_copy(
            src_ref=src, dst_ref=dst, send_sem=s, recv_sem=r, device_id=peer, device_id_type=MESH
        )

    @pl.loop(1, 8)
    def _(d):
        t = (u + d) % 8
        remote(msg.at[t], mid.at[d], p1_s, p1_r, device_of(t, v)).start()

    top, bottom = pl.ds(H - 1, 1), pl.ds(0, 1)
    low, high = pl.ds(EH - 1, 1), pl.ds(H, 1)
    wide = pl.ds(0, W)
    edge = [
        remote(di_hbm.at[1, :, top], dx.at[1, :, low, wide], ns_s.at[0], ns_r.at[0], north),
        remote(ve_hbm.at[1, :, top], vx.at[1, :, low, wide], ns_s.at[1], ns_r.at[1], north),
        remote(wet_hbm.at[:, top], wi.at[:, low], ns_s.at[2], ns_r.at[2], north),
        remote(wet_hbm.at[:, bottom], wi.at[:, high], ns_s.at[3], ns_r.at[3], south),
    ]
    for i, peer in enumerate((east, west, north, south)):
        edge.append(remote(fsend.at[1 + i], fgot.at[i], fl_s.at[i], fl_r.at[i], peer))
    for copy in edge:
        copy.start()
    mid[0] = msg[u]

    for copy in loads:
        copy.wait()

    lane64 = iota((H, 128), 1)

    def planes_of(t):
        for q in range(20):
            n, k = q // LEVELS, q % LEVELS
            yield q, ((c0, (n, k)), (dx, (0, k)) if n == 0 else (vx, (0, k)), (dx, (1, k)) if n == 0 else (vx, (1, k)), (dx, (2, k)) if n == 0 else (wf, (k,)))[t]

    for k in range(LEVELS):
        wf[k, pl.ds(0, H), wide] = wi[k, pl.ds(0, H)].astype(F32)
    for t in range(4):
        acc = jnp.zeros((H, 128), F32)
        for q, (ref, at) in planes_of(t):
            left = ref[at + (pl.ds(0, H), pl.ds(0, 128))]
            right = ref[at + (pl.ds(0, H), pl.ds(384, 128))]
            both = pltpu.roll(jnp.where(lane64 < 3, left, right), 6 * q + 3, 1)
            acc = jnp.where(lane64 >= 6 * q, both, acc)
        packs[t] = acc
    sides = [
        remote(packs, from_w, ew_s.at[0], ew_r.at[0], east),
        remote(packs, from_e, ew_s.at[1], ew_r.at[1], west),
        remote(packs.at[:, pl.ds(56, 8)], from_sw, ew_s.at[2], ew_r.at[2], ne),
        remote(packs.at[:, pl.ds(56, 8)], from_se, ew_s.at[3], ew_r.at[3], nw),
        remote(packs.at[:, pl.ds(0, 8)], from_nw, ew_s.at[4], ew_r.at[4], se),
        remote(packs.at[:, pl.ds(0, 8)], from_ne, ew_s.at[5], ew_r.at[5], sw),
    ]
    for copy in sides:
        copy.start()

    done = remote(mid.at[pl.ds(1, 7)], mid.at[pl.ds(1, 7)], p1_s, p1_r, east)
    done.wait_send()
    done.wait_recv()

    @pl.loop(1, 16)
    def _(d):
        t = (v + d) % 16
        remote(mid.at[:, t // 4, t % 4], got.at[d], p2_s, p2_r, device_of(u, t)).start()

    got[0] = mid[:, v // 4, v % 4]

    sub8 = iota((8, EW), 0)

    def up(cur, nxt):
        n = cur.shape[1]
        return jnp.where(sub8[:, :n] == 7, pltpu.roll(nxt, 7, 0), pltpu.roll(cur, 7, 0))

    def coefficients(k, strip, a, b):
        rows = pl.ds(8 * strip, 8)
        after = pl.ds(8 * ((strip + 1) % STRIPS), 8)
        lanes = pl.ds(a, b - a)
        w = wf[k, rows, lanes]
        if b < EW:
            w_e = pltpu.roll(wf[k, rows, pl.ds(a, b - a + 128)], b - a + 127, 1)[:, : b - a]
        elif a == 0:
            w_e = pltpu.roll(w, EW - 1, 1)
        else:
            w_e = jnp.concatenate([w, wf[k, rows, pl.ds(0, 128)]], axis=1)
            w_e = pltpu.roll(w_e, b - a + 127, 1)[:, : b - a]
        w_n = up(w, wf[k, after, lanes])
        w_v = wf[k + 1, rows, lanes]
        for i, other in ((0, w_e), (1, w_n)):
            if strip == 8 and i == 0:
                continue
            d, f, open_ = dx[i, k, rows, lanes], 0.5 * vx[i, k, rows, lanes], w * other
            dx[i, k, rows, lanes] = open_ * (d - f)
            vx[i, k, rows, lanes] = open_ * (d + f)
        if strip < 8:
            dx[2, k, rows, lanes] = w * w_v * dx[2, k, rows, lanes]

    wf[LEVELS] = jnp.zeros((EH, EW), F32)
    for n in range(2):
        c0[n, LEVELS] = jnp.zeros((EH, EW), F32)
        c1[n, LEVELS] = jnp.zeros((EH, EW), F32)

    @pl.loop(0, LEVELS)
    def _(k):
        for strip in range(7):
            coefficients(k, strip, 0, 384)

    spread_lane = iota((128, 128), 1)
    within = spread_lane % 6
    picked = spread_lane // 6
    inner = spread_lane < 120
    for b, start in enumerate((0, PAY, 4 * PAY, 5 * PAY)):
        hit = (iota((128, 128), 0) == start + picked) & inner
        spread[:, pl.ds(128 * b, 128)] = jnp.where(hit, 1.0, 0.0).astype(BF16)
    targets = (
        jnp.where((within < 3) & inner, 509 + within, -1), jnp.where((within >= 3) & inner, within - 3, -1)
    )

    for i in range(4):
        edge[4 + i].wait()
    blocks = [fsend[0]] + [fgot[i] for i in range(4)]
    reach = {3: jnp.where(lat > 0, 1.0, 0.0), 4: jnp.where(lat < 3, 1.0, 0.0)}
    cells = iota((W, 128), 0)
    lows, fracs = [], []
    for g in range(5):
        for s in range(4):
            xpos = blocks[g][s : s + 1, 256:384] * (W - 1.0)
            lowest = jnp.clip(jnp.floor(xpos).astype(I32), 0, W - 2)
            fracs.append(xpos - lowest.astype(F32))
            hot[:, pl.ds(512 * g + 128 * s, 128)] = jnp.where(cells == lowest, 1.0, 0.0).astype(BF16)

    for copy in edge[:4] + sides:
        copy.wait()
    inside = jnp.where(iota((8, W), 0) < 4, jnp.where(lat < 3, 1, 0), jnp.where(lat > 0, 1, 0))
    for k in range(LEVELS):
        wf[k, pl.ds(H, 8), wide] = jnp.where(inside > 0, wi[k, pl.ds(H, 8)].astype(F32), 0.0)
    lane8 = iota((8, 128), 1)
    side = []
    for t in range(4):
        body = jnp.where(lane64 % 6 < 3, from_w[t], from_e[t])
        upper = jnp.where(lane8 % 6 < 3, from_nw[t], from_ne[t])
        lower = jnp.where(lane8 % 6 < 3, from_sw[t], from_se[t])
        side.append(jnp.concatenate([body, jnp.where(sub8[:, :128] < 4, upper, lower)], axis=0))

    def unpack(t, q, ref, at):
        values = pltpu.roll(side[t], (128 - 6 * q - 3) % 128, 1)
        if ref is wf:
            edge_rows = jnp.where(inside[:, :128] > 0, values[H:], 0.0)
            values = jnp.concatenate([values[:H], edge_rows], axis=0)
        return ref, at, values

    def unpack_all(blocks_of):
        held = []
        for t in blocks_of:
            for q, (ref, at) in planes_of(t):
                held.append(unpack(t, q, ref, at))
                if len(held) > 3:
                    ref, at, values = held.pop(0)
                    ref[at + (pl.ds(0, values.shape[0]), pl.ds(W, 128))] = values
        for ref, at, values in held:
            ref[at + (pl.ds(0, values.shape[0]), pl.ds(W, 128))] = values

    unpack_all((1, 2, 3))

    @pl.loop(0, LEVELS)
    def _(k):
        for strip in range(7):
            coefficients(k, strip, 384, EW)
        coefficients(k, 7, 0, EW)
        coefficients(k, 8, 0, EW)

    done = remote(got.at[pl.ds(1, 15)], got.at[pl.ds(1, 15)], p2_s, p2_r, east)
    done.wait_send()
    done.wait_recv()

    rims = {}

    def exchange(ref, number):
        def rim(a, b, i, peer):
            at = [ref.at[:, pl.ds(0, LEVELS), pl.ds(r, 1)] for r in (a, b)]
            return remote(at[0], at[1], row_s.at[2 * number + i], row_r.at[2 * number + i], peer)

        rims[number] = rim(H - 1, EH - 1, 0, north), rim(0, H, 1, south)
        for copy in rims[number]:
            copy.start()

    vals = got[...].reshape(128, 128)
    valsT = vals.T
    cols = (vals.astype(I32) - 1) & (W - 1)
    rowsT = (valsT.astype(I32) - 1) >> 9

    grown = [jnp.dot(part, spread[...], preferred_element_type=F32) for part in split(vals)]
    sub64 = iota((H, 128), 0)
    pick, hi_parts, lo_parts, ones = [], [], [], []
    for b, start in enumerate((0, PAY, 4 * PAY, 5 * PAY)):
        at = start + PAY - 1
        pick.append(jnp.where(sub64 == rowsT[at : at + 1], 1.0, 0.0))
        match = jnp.where(cols[:, at : at + 1] == targets[b // 2], 1.0, 0.0)
        hi_parts.append(match * grown[0][:, 128 * b : 128 * b + 128])
        lo_parts.append(match * grown[1][:, 128 * b : 128 * b + 128])
        ones.append(match)
    pick = jnp.concatenate(pick, axis=1).astype(BF16)
    onto = jnp.concatenate([jnp.concatenate(p, axis=0).astype(BF16) for p in (hi_parts, lo_parts, ones)], axis=1)
    beside = jnp.dot(pick, onto, preferred_element_type=F32)

    wide_lane = iota((128, W), 1)
    slots = (2 * PAY, 3 * PAY)
    own_rows = jnp.concatenate([rowsT[b + PAY - 1 : b + PAY] for b in slots], axis=1)
    own = jnp.where(iota((H, 256), 0) == own_rows, 1.0, 0.0)
    for c in range(20):
        value = jnp.concatenate([valsT[b + c : b + c + 1] for b in slots], axis=1)
        value_hi = value.astype(BF16).astype(F32)
        amat[pl.ds(H * c, H), pl.ds(0, 256)] = (own * value_hi).astype(BF16)
        amat[pl.ds(H * c, H), pl.ds(256, 256)] = (own * (value - value_hi)).astype(BF16)
    amat[pl.ds(H * 20, H), pl.ds(0, 256)] = own.astype(BF16)
    amat[pl.ds(H * 20, H), pl.ds(256, 256)] = jnp.zeros((H, 256), BF16)
    onto = [jnp.where(wide_lane == cols[:, b + PAY - 1 : b + PAY], 1.0, 0.0) for b in slots]
    onto = jnp.concatenate(onto + onto, axis=0).astype(BF16)
    added = jnp.dot(amat[...], onto, preferred_element_type=F32)
    keep = 1.0 - 0.5 * added[H * 20 :]
    for c in range(20):
        at = (c // LEVELS, c % LEVELS, pl.ds(0, H), wide)
        c0[at] = c0[at] * keep + added[H * c : H * c + H]
    body = side[0][:H]
    side[0] = body * (1.0 - 0.5 * beside[:, 256:384]) + beside[:, 0:128] + beside[:, 128:256]

    unpack_all((0,))
    exchange(c0, 0)

    tiles = EW // 128
    first_lane, last_lane = iota((8, 128), 1) == 0, iota((8, 128), 1) == 127
    first_row, last_row = iota((8, 128), 0) == 0, iota((8, 128), 0) == 7

    def sweep(src, dst, last, starts):
        @pl.loop(0, LEVELS)
        def _(k):
            def load(ref, at, i):
                return [ref[at + (pl.ds(8 * (i % STRIPS), 8), pl.ds(128 * j, 128))] for j in range(tiles)]

            started, fluxes, turned, below = {}, {}, {}, {}

            def start(i, n):
                here = load(src, (n, k), i)
                started[i, n] = here, [pltpu.roll(x, 127, 1) for x in here]

            def face(i, n):
                here, moved = started.pop((i, n))
                east_of = [jnp.where(last_lane, moved[(j + 1) % tiles], moved[j]) for j in range(tiles)]
                flux = [
                    a * x - b * y for a, b, x, y in zip(load(dx, (0, k), i), load(vx, (0, k), i), east_of, here)
                ]
                fluxes[i, n] = here, flux, [pltpu.roll(x, 1, 1) for x in flux]

            def north_flux(i, here, above):
                return [a * x - b * y for a, b, x, y in zip(load(dx, (1, k), i), load(vx, (1, k), i), above, here)]

            def finish(i, n):
                here, flux, moved = fluxes.pop((i, n))
                lifted = [pltpu.roll(x, 7, 0) for x in load(src, (n, k), i + 1)]
                above = [jnp.where(last_row, a, b) for a, b in zip(lifted, turned[i, n])]
                flux_n = north_flux(i, here, above)
                dropped = [pltpu.roll(x, 1, 0) for x in flux_n]
                higher = load(src, (n, k + 1), i)
                flux_v = [c * (x - y) for c, x, y in zip(load(dx, (2, k), i), higher, here)]
                flux_u = load(vbuf, (n,), i)
                rows = pl.ds(8 * i, 8)
                for j in range(tiles):
                    vbuf[n, rows, pl.ds(128 * j, 128)] = flux_v[j]
                    if last and j == tiles - 1:
                        continue
                    new = here[j] + (flux_n[j] - jnp.where(first_row, below[i, n][j], dropped[j]))
                    new = new + (flux[j] - jnp.where(first_lane, moved[j - 1], moved[j])) + (flux_v[j] - flux_u[j])
                    dst[n, k, rows, pl.ds(128 * j, 128)] = new
                turned[i + 1, n], below[i + 1, n] = lifted, dropped

            chunks = []
            for first, count in starts:
                for n in range(2):
                    prev = (first - 1) % STRIPS
                    tail, head = load(src, (n, k), prev), load(src, (n, k), first)
                    turned[first, n] = [pltpu.roll(x, 7, 0) for x in head]
                    above = [jnp.where(last_row, a, pltpu.roll(b, 7, 0)) for a, b in zip(turned[first, n], tail)]
                    below[first, n] = [pltpu.roll(x, 1, 0) for x in north_flux(prev, tail, above)]
                chunks += [(first + i, n) for i in range(count) for n in range(2)]
            for at in range(len(chunks) + 2 * GAP):
                for stage, work in enumerate((start, face, finish)):
                    if 0 <= at - stage * GAP < len(chunks):
                        work(*chunks[at - stage * GAP])

    for number, (src, dst) in enumerate(((c0, c1), (c1, c0), (c0, out_ref))):
        vbuf[...] = jnp.zeros((2, EH, EW), F32)
        sweep(src, dst, number == 2, [(1, 6)])
        for copy in rims[number]:
            copy.wait()
        sweep(src, dst, number == 2, [(7, 1), (0, 1)])
        if number < 2:
            exchange(dst, number + 1)

    plane = jnp.concatenate([out_ref[0, 0], out_ref[1, 0]], axis=0)
    nexts = pltpu.roll(plane, W - 1, 1)
    lhs = jnp.concatenate(list(split(plane)) + list(split(nexts)), axis=0)
    line = iota((H, 128), 0).astype(F32)
    for g in range(5):
        res = jnp.dot(lhs, hot[:, pl.ds(512 * g, 512)], preferred_element_type=F32)
        for s in range(4):
            part = res[:, 128 * s : 128 * s + 128]
            frac = fracs[4 * g + s]
            along = (1.0 - frac) * (part[0:128] + part[128:256]) + frac * (part[256:384] + part[384:512])
            ypos = blocks[g][s : s + 1, 384:512] * (H - 1.0)
            tent = jnp.maximum(0.0, 1.0 - jnp.abs(ypos - line))
            flag = blocks[g][s : s + 1, 512:640]
            for n in range(2):
                sample = jnp.sum(along[H * n : H * n + H] * tent, axis=0, keepdims=True)
                value = flag * (0.5 * blocks[g][s : s + 1, 128 * n : 128 * n + 128] + 0.5 * sample)
                if g in reach:
                    value = reach[g] * value
                fout_ref[4 * g + s, pl.ds(n, 1), :] = value


def shards(tracers, diffusivity, velocity, wet_mask, argo_rows, argo_dest, argo_cols, argo_count, float_values, float_pos, float_dest):
    vmem = pl.BlockSpec(memory_space=pltpu.VMEM)
    hbm = pl.BlockSpec(memory_space=pl.ANY)
    smem = pl.BlockSpec(memory_space=pltpu.SMEM)
    dma, scratch = pltpu.SemaphoreType.DMA, pltpu.VMEM
    return pl.pallas_call(
        kernel,
        out_shape=(
            jax.ShapeDtypeStruct(tracers.shape, F32),
            jax.ShapeDtypeStruct((20, 2, 128), F32),
        ),
        in_specs=[hbm] * 4 + [vmem, vmem, vmem, smem, vmem, vmem, vmem],
        out_specs=(vmem, vmem),
        scratch_shapes=[
            scratch((2, LEVELS + 1, EH, EW), F32),
            scratch((2, LEVELS + 1, EH, EW), F32),
            scratch((3, LEVELS, EH, EW), F32),
            scratch((2, LEVELS, EH, EW), F32),
            scratch((LEVELS, EH, W), I32),
            scratch((LEVELS + 1, EH, EW), F32),
            scratch((2, EH, EW), F32),
            scratch((4, H, 128), F32),
            scratch((4, H, 128), F32),
            scratch((4, H, 128), F32),
            scratch((4, 8, 128), F32),
            scratch((4, 8, 128), F32),
            scratch((4, 8, 128), F32),
            scratch((4, 8, 128), F32),
            scratch((8, 4, 4, 1, 128), F32),
            scratch((8, 4, 4, 1, 128), F32),
            scratch((16, 8, 1, 128), F32),
            scratch((5, 8, 640), F32),
            scratch((4, 8, 640), F32),
            scratch((H * 21, 512), BF16),
            scratch((W, 2560), BF16),
            scratch((128, 512), BF16),
            dma((4,)), dma, dma, dma, dma, dma((4,)), dma((4,)), dma((6,)), dma((6,)), dma((4,)), dma((4,)),
            dma((6,)), dma((6,)),
        ],
        compiler_params=pltpu.CompilerParams(
            collective_id=1, has_side_effects=True, vmem_limit_bytes=60 * 1024 * 1024
        ),
    )(
        tracers, diffusivity, velocity, wet_mask, argo_rows, argo_dest.reshape(1, -1), argo_cols.reshape(1, -1),
        argo_count, float_values, float_pos, float_dest.reshape(1, -1),
    )


def solution(mesh):
    grid4, grid3 = P(None, None, "lat", "lon"), P(None, "lat", "lon")
    tiles = ("lon", "lat")
    return jax.shard_map(
        shards,
        mesh=mesh,
        in_specs=(
            grid4, grid4, grid4, grid3, P(tiles, None), P(tiles, None), P(tiles), P(tiles),
            P(tiles, None, None), P(tiles, None, None), P(tiles, None),
        ),
        out_specs=(grid4, P(tiles, None, None)),
        check_vma=False,
    )
```

```python
import functools

import jax
import jax.numpy as jnp
from jax import lax
from jax.experimental import pallas as pl
from jax.experimental.pallas import tpu as pltpu
from jax.sharding import PartitionSpec as P

MESH = pl.DeviceIdType.MESH
F32, BF16, I32 = jnp.float32, jnp.bfloat16, jnp.int32

LEVELS, H, W = 10, 64, 512
EH, EW = 72, 640
STRIPS = EH // 8
GAP = 3
PAY = 21


def split(x):
    high = x.astype(BF16)
    return high, (x - high.astype(F32)).astype(BF16)


def iota(shape, dim):
    return lax.broadcasted_iota(I32, shape, dim)


def column_of(row):
    n = row.shape[1]
    wide = jnp.broadcast_to(row, (n, n))
    return jnp.sum(jnp.where(iota((n, n), 0) == iota((n, n), 1), wide, 0.0), axis=1, keepdims=True)


def ranks_of(row):
    n = row.shape[1]
    earlier = (column_of(row) == row) & (iota((n, n), 0) < iota((n, n), 1))
    return jnp.sum(earlier.astype(F32), axis=0, keepdims=True)


def places():
    lon, lat = lax.axis_index("lon"), lax.axis_index("lat")
    z, b = lon % 4, lon // 4
    u, v = (b % 2) * 4 + lat, (b // 2) * 4 + z
    return lon, lat, u, v


def device_of(u, v):
    return ((v // 4) * 8 + (u // 4) * 4 + v % 4, u % 4)


def kernel(
    tr_hbm, di_hbm, ve_hbm, wet_hbm, rows_hbm, dest_hbm, cols_hbm, count_hbm, fval_hbm, fpos_hbm, fdest_hbm,
    out_ref, fout_ref,
    c0, c1, dx, vx, wi, wf, vbuf, packs, from_w, from_e, from_nw, from_sw, from_ne, from_se,
    msg, mid, got, fsend, fgot, amat, hot, spread,
    rows_ref, dest_ref, cols_ref, count_ref, fval_ref, fpos_ref, fdest_ref,
    small_sem, load_sem, p1_s, p1_r, p2_s, p2_r, ns_s, ns_r, ew_s, ew_r, fl_s, fl_r, row_s, row_r,
):
    lon, lat, u, v = places()
    east, west = ((lon + 1) % 32, lat), ((lon + 31) % 32, lat)
    north, south = (lon, (lat + 1) % 4), (lon, (lat + 3) % 4)
    ne, se = (east[0], north[1]), (east[0], south[1])
    nw, sw = (west[0], north[1]), (west[0], south[1])
    barrier = pltpu.get_barrier_semaphore()

    smalls = [
        pltpu.make_async_copy(src, dst, small_sem.at[i])
        for i, (src, dst) in enumerate((
            (rows_hbm, rows_ref), (dest_hbm, dest_ref), (cols_hbm, cols_ref), (count_hbm, count_ref),
            (fval_hbm, fval_ref), (fpos_hbm, fpos_ref), (fdest_hbm, fdest_ref),
        ))
    ]
    for copy in smalls:
        copy.start()

    @pl.loop(1, 8)
    def _(d):
        pl.semaphore_signal(barrier, inc=1, device_id=device_of((u + d) % 8, v), device_id_type=MESH)

    @pl.loop(1, 16)
    def _(d):
        pl.semaphore_signal(barrier, inc=1, device_id=device_of(u, (v + d) % 16), device_id_type=MESH)

    for peer in (east, west, north, south, ne, se, nw, sw):
        pl.semaphore_signal(barrier, inc=1, device_id=peer, device_id_type=MESH)

    loads = [
        pltpu.make_async_copy(di_hbm, dx.at[:, :, pl.ds(0, H), pl.ds(0, W)], load_sem.at[0]),
        pltpu.make_async_copy(ve_hbm, vx.at[:, :, pl.ds(0, H), pl.ds(0, W)], load_sem.at[1]),
        pltpu.make_async_copy(wet_hbm, wi.at[:, pl.ds(0, H)], load_sem.at[2]),
        pltpu.make_async_copy(tr_hbm, c0.at[:, pl.ds(0, LEVELS), pl.ds(0, H), pl.ds(0, W)], load_sem.at[3]),
    ]
    for copy in loads:
        copy.start()

    for copy in smalls:
        copy.wait()

    lane = iota((128, 128), 1)
    sub = iota((128, 128), 0)
    level = jnp.where(sub >= PAY, sub - PAY, sub)
    tracer = jnp.where(level >= LEVELS, 1, 0)
    level = level - tracer * LEVELS
    depth = lane - tracer * 64
    weight = jnp.maximum(0.0, 1.0 - jnp.abs(depth.astype(F32) * ((LEVELS - 1) / 63.0) - level.astype(F32)))
    weight = jnp.where((depth >= 0) & (depth < 64), weight, 0.0)
    total = jnp.sum(weight, axis=1, keepdims=True)
    table = 0.5 * weight / jnp.where(total > 0.0, total, 1.0)
    pay = lax.dot_general(
        table, rows_ref[...], (((1,), (1,)), ((), ())), precision=lax.Precision.HIGHEST, preferred_element_type=F32
    )
    cell = (cols_ref[...] + 1).astype(F32)
    pay = jnp.where((sub == PAY - 1) | (sub == 2 * PAY - 1), jnp.broadcast_to(cell, (128, 128)), pay)
    pay = jnp.concatenate([jnp.where(sub < PAY, pay, 0.0), jnp.where((sub >= PAY) & (sub < 2 * PAY), pay, 0.0)], axis=1)
    live = iota((1, 128), 1) < count_ref[0]
    dest = jnp.where(live, dest_ref[...], -5).astype(F32)
    rank = ranks_of(dest)
    tile = ((sub % 32) * 4 + sub // 32).astype(F32)
    first = jnp.where((tile == dest) & (rank == 0.0), 1.0, 0.0)
    second = jnp.where((tile == dest) & (rank == 1.0), 1.0, 0.0)
    chosen = jnp.concatenate([first, second], axis=1).astype(BF16)
    ordered = sum(
        lax.dot_general(chosen, part, (((1,), (1,)), ((), ())), preferred_element_type=F32) for part in split(pay)
    )
    for b in range(4):
        mine = ordered[32 * b : 32 * b + 32]
        full = pltpu.roll(mine, 1, 0) + pltpu.roll(mine, 2 * PAY, 1) + pltpu.roll(pltpu.roll(mine, 31, 0), 4 * PAY, 1)
        for h in range(2):
            for y in range(4):
                for z in range(4):
                    at = 8 * y + 4 * h + z
                    msg[4 * h + b, y, z] = full[at : at + 1]

    fdest = fdest_ref[...].astype(F32)
    place = 8.0 * fdest + ranks_of(fdest)
    fhot = (iota((40, 16), 0).astype(F32) == place).astype(F32)
    fpay = jnp.concatenate([fval_ref[:, 0], fval_ref[:, 1], fpos_ref[:, 0], fpos_ref[:, 1]], axis=1)
    fordered = jnp.dot(fhot, fpay, precision=lax.Precision.HIGHEST, preferred_element_type=F32)
    fsend[:, :, pl.ds(0, 512)] = fordered.reshape(5, 8, 512)
    flags = jnp.broadcast_to(jnp.sum(fhot, axis=1, keepdims=True), (40, 128))
    fsend[:, :, pl.ds(512, 128)] = flags.reshape(5, 8, 128)

    pl.semaphore_wait(barrier, 30)

    def remote(src, dst, s, r, peer):
        return pltpu.make_async_remote_copy(
            src_ref=src, dst_ref=dst, send_sem=s, recv_sem=r, device_id=peer, device_id_type=MESH
        )

    @pl.loop(1, 8)
    def _(d):
        t = (u + d) % 8
        remote(msg.at[t], mid.at[d], p1_s, p1_r, device_of(t, v)).start()

    top, bottom = pl.ds(H - 1, 1), pl.ds(0, 1)
    low, high = pl.ds(EH - 1, 1), pl.ds(H, 1)
    wide = pl.ds(0, W)
    edge = [
        remote(di_hbm.at[1, :, top], dx.at[1, :, low, wide], ns_s.at[0], ns_r.at[0], north),
        remote(ve_hbm.at[1, :, top], vx.at[1, :, low, wide], ns_s.at[1], ns_r.at[1], north),
        remote(wet_hbm.at[:, top], wi.at[:, low], ns_s.at[2], ns_r.at[2], north),
        remote(wet_hbm.at[:, bottom], wi.at[:, high], ns_s.at[3], ns_r.at[3], south),
    ]
    for i, peer in enumerate((east, west, north, south)):
        edge.append(remote(fsend.at[1 + i], fgot.at[i], fl_s.at[i], fl_r.at[i], peer))
    for copy in edge:
        copy.start()
    mid[0] = msg[u]

    for copy in loads:
        copy.wait()

    lane64 = iota((H, 128), 1)

    def planes_of(t):
        for q in range(20):
            n, k = q // LEVELS, q % LEVELS
            yield q, ((c0, (n, k)), (dx, (0, k)) if n == 0 else (vx, (0, k)), (dx, (1, k)) if n == 0 else (vx, (1, k)), (dx, (2, k)) if n == 0 else (wf, (k,)))[t]

    for k in range(LEVELS):
        wf[k, pl.ds(0, H), wide] = wi[k, pl.ds(0, H)].astype(F32)
    for t in range(4):
        acc = jnp.zeros((H, 128), F32)
        for q, (ref, at) in planes_of(t):
            left = ref[at + (pl.ds(0, H), pl.ds(0, 128))]
            right = ref[at + (pl.ds(0, H), pl.ds(384, 128))]
            both = pltpu.roll(jnp.where(lane64 < 3, left, right), 6 * q + 3, 1)
            acc = jnp.where(lane64 >= 6 * q, both, acc)
        packs[t] = acc
    sides = [
        remote(packs, from_w, ew_s.at[0], ew_r.at[0], east),
        remote(packs, from_e, ew_s.at[1], ew_r.at[1], west),
        remote(packs.at[:, pl.ds(56, 8)], from_sw, ew_s.at[2], ew_r.at[2], ne),
        remote(packs.at[:, pl.ds(56, 8)], from_se, ew_s.at[3], ew_r.at[3], nw),
        remote(packs.at[:, pl.ds(0, 8)], from_nw, ew_s.at[4], ew_r.at[4], se),
        remote(packs.at[:, pl.ds(0, 8)], from_ne, ew_s.at[5], ew_r.at[5], sw),
    ]
    for copy in sides:
        copy.start()

    done = remote(mid.at[pl.ds(1, 7)], mid.at[pl.ds(1, 7)], p1_s, p1_r, east)
    done.wait_send()
    done.wait_recv()

    @pl.loop(1, 16)
    def _(d):
        t = (v + d) % 16
        remote(mid.at[:, t // 4, t % 4], got.at[d], p2_s, p2_r, device_of(u, t)).start()

    got[0] = mid[:, v // 4, v % 4]

    sub8 = iota((8, EW), 0)

    def up(cur, nxt):
        n = cur.shape[1]
        return jnp.where(sub8[:, :n] == 7, pltpu.roll(nxt, 7, 0), pltpu.roll(cur, 7, 0))

    def coefficients(k, strip, a, b):
        rows = pl.ds(8 * strip, 8)
        after = pl.ds(8 * ((strip + 1) % STRIPS), 8)
        lanes = pl.ds(a, b - a)
        w = wf[k, rows, lanes]
        if b < EW:
            w_e = pltpu.roll(wf[k, rows, pl.ds(a, b - a + 128)], b - a + 127, 1)[:, : b - a]
        elif a == 0:
            w_e = pltpu.roll(w, EW - 1, 1)
        else:
            w_e = jnp.concatenate([w, wf[k, rows, pl.ds(0, 128)]], axis=1)
            w_e = pltpu.roll(w_e, b - a + 127, 1)[:, : b - a]
        w_n = up(w, wf[k, after, lanes])
        w_v = wf[k + 1, rows, lanes]
        for i, other in ((0, w_e), (1, w_n)):
            if strip == 8 and i == 0:
                continue
            d, f, open_ = dx[i, k, rows, lanes], 0.5 * vx[i, k, rows, lanes], w * other
            dx[i, k, rows, lanes] = open_ * (d - f)
            vx[i, k, rows, lanes] = open_ * (d + f)
        if strip < 8:
            dx[2, k, rows, lanes] = w * w_v * dx[2, k, rows, lanes]

    wf[LEVELS] = jnp.zeros((EH, EW), F32)
    for n in range(2):
        c0[n, LEVELS] = jnp.zeros((EH, EW), F32)
        c1[n, LEVELS] = jnp.zeros((EH, EW), F32)

    @pl.loop(0, LEVELS)
    def _(k):
        for strip in range(7):
            coefficients(k, strip, 0, 384)

    spread_lane = iota((128, 128), 1)
    within = spread_lane % 6
    picked = spread_lane // 6
    inner = spread_lane < 120
    for b, start in enumerate((0, PAY, 4 * PAY, 5 * PAY)):
        hit = (iota((128, 128), 0) == start + picked) & inner
        spread[:, pl.ds(128 * b, 128)] = jnp.where(hit, 1.0, 0.0).astype(BF16)
    targets = (
        jnp.where((within < 3) & inner, 509 + within, -1), jnp.where((within >= 3) & inner, within - 3, -1)
    )

    for i in range(4):
        edge[4 + i].wait()
    blocks = [fsend[0]] + [fgot[i] for i in range(4)]
    reach = {3: jnp.where(lat > 0, 1.0, 0.0), 4: jnp.where(lat < 3, 1.0, 0.0)}
    cells = iota((W, 128), 0)
    lows, fracs = [], []
    for g in range(5):
        for s in range(4):
            xpos = blocks[g][s : s + 1, 256:384] * (W - 1.0)
            lowest = jnp.clip(jnp.floor(xpos).astype(I32), 0, W - 2)
            fracs.append(xpos - lowest.astype(F32))
            hot[:, pl.ds(512 * g + 128 * s, 128)] = jnp.where(cells == lowest, 1.0, 0.0).astype(BF16)

    for copy in edge[:4] + sides:
        copy.wait()
    inside = jnp.where(iota((8, W), 0) < 4, jnp.where(lat < 3, 1, 0), jnp.where(lat > 0, 1, 0))
    for k in range(LEVELS):
        wf[k, pl.ds(H, 8), wide] = jnp.where(inside > 0, wi[k, pl.ds(H, 8)].astype(F32), 0.0)
    lane8 = iota((8, 128), 1)
    side = []
    for t in range(4):
        body = jnp.where(lane64 % 6 < 3, from_w[t], from_e[t])
        upper = jnp.where(lane8 % 6 < 3, from_nw[t], from_ne[t])
        lower = jnp.where(lane8 % 6 < 3, from_sw[t], from_se[t])
        side.append(jnp.concatenate([body, jnp.where(sub8[:, :128] < 4, upper, lower)], axis=0))

    def unpack(t, q, ref, at):
        values = pltpu.roll(side[t], (128 - 6 * q - 3) % 128, 1)
        if ref is wf:
            edge_rows = jnp.where(inside[:, :128] > 0, values[H:], 0.0)
            values = jnp.concatenate([values[:H], edge_rows], axis=0)
        return ref, at, values

    def unpack_all(blocks_of):
        held = []
        for t in blocks_of:
            for q, (ref, at) in planes_of(t):
                held.append(unpack(t, q, ref, at))
                if len(held) > 3:
                    ref, at, values = held.pop(0)
                    ref[at + (pl.ds(0, values.shape[0]), pl.ds(W, 128))] = values
        for ref, at, values in held:
            ref[at + (pl.ds(0, values.shape[0]), pl.ds(W, 128))] = values

    unpack_all((1, 2, 3))

    @pl.loop(0, LEVELS)
    def _(k):
        for strip in range(7):
            coefficients(k, strip, 384, EW)
        coefficients(k, 7, 0, EW)
        coefficients(k, 8, 0, EW)

    done = remote(got.at[pl.ds(1, 15)], got.at[pl.ds(1, 15)], p2_s, p2_r, east)
    done.wait_send()
    done.wait_recv()

    rims = {}

    def exchange(ref, number):
        def rim(a, b, i, peer):
            at = [ref.at[:, pl.ds(0, LEVELS), pl.ds(r, 1)] for r in (a, b)]
            return remote(at[0], at[1], row_s.at[2 * number + i], row_r.at[2 * number + i], peer)

        rims[number] = rim(H - 1, EH - 1, 0, north), rim(0, H, 1, south)
        for copy in rims[number]:
            copy.start()

    vals = got[...].reshape(128, 128)
    valsT = vals.T
    cols = (vals.astype(I32) - 1) & (W - 1)
    rowsT = (valsT.astype(I32) - 1) >> 9

    grown = [jnp.dot(part, spread[...], preferred_element_type=F32) for part in split(vals)]
    sub64 = iota((H, 128), 0)
    pick, hi_parts, lo_parts, ones = [], [], [], []
    for b, start in enumerate((0, PAY, 4 * PAY, 5 * PAY)):
        at = start + PAY - 1
        pick.append(jnp.where(sub64 == rowsT[at : at + 1], 1.0, 0.0))
        match = jnp.where(cols[:, at : at + 1] == targets[b // 2], 1.0, 0.0)
        hi_parts.append(match * grown[0][:, 128 * b : 128 * b + 128])
        lo_parts.append(match * grown[1][:, 128 * b : 128 * b + 128])
        ones.append(match)
    pick = jnp.concatenate(pick, axis=1).astype(BF16)
    onto = jnp.concatenate([jnp.concatenate(p, axis=0).astype(BF16) for p in (hi_parts, lo_parts, ones)], axis=1)
    beside = jnp.dot(pick, onto, preferred_element_type=F32)

    wide_lane = iota((128, W), 1)
    slots = (2 * PAY, 3 * PAY)
    own_rows = jnp.concatenate([rowsT[b + PAY - 1 : b + PAY] for b in slots], axis=1)
    own = jnp.where(iota((H, 256), 0) == own_rows, 1.0, 0.0)
    for c in range(20):
        value = jnp.concatenate([valsT[b + c : b + c + 1] for b in slots], axis=1)
        value_hi = value.astype(BF16).astype(F32)
        amat[pl.ds(H * c, H), pl.ds(0, 256)] = (own * value_hi).astype(BF16)
        amat[pl.ds(H * c, H), pl.ds(256, 256)] = (own * (value - value_hi)).astype(BF16)
    amat[pl.ds(H * 20, H), pl.ds(0, 256)] = own.astype(BF16)
    amat[pl.ds(H * 20, H), pl.ds(256, 256)] = jnp.zeros((H, 256), BF16)
    onto = [jnp.where(wide_lane == cols[:, b + PAY - 1 : b + PAY], 1.0, 0.0) for b in slots]
    onto = jnp.concatenate(onto + onto, axis=0).astype(BF16)
    added = jnp.dot(amat[...], onto, preferred_element_type=F32)
    keep = 1.0 - 0.5 * added[H * 20 :]
    for c in range(20):
        at = (c // LEVELS, c % LEVELS, pl.ds(0, H), wide)
        c0[at] = c0[at] * keep + added[H * c : H * c + H]
    body = side[0][:H]
    side[0] = body * (1.0 - 0.5 * beside[:, 256:384]) + beside[:, 0:128] + beside[:, 128:256]

    unpack_all((0,))
    exchange(c0, 0)

    tiles = EW // 128
    first_lane, last_lane = iota((8, 128), 1) == 0, iota((8, 128), 1) == 127
    first_row, last_row = iota((8, 128), 0) == 0, iota((8, 128), 0) == 7

    def sweep(src, dst, last, starts):
        @pl.loop(0, LEVELS)
        def _(k):
            def load(ref, at, i):
                return [ref[at + (pl.ds(8 * (i % STRIPS), 8), pl.ds(128 * j, 128))] for j in range(tiles)]

            started, fluxes, turned, below = {}, {}, {}, {}

            def start(i, n):
                here = load(src, (n, k), i)
                started[i, n] = here, [pltpu.roll(x, 127, 1) for x in here]

            def face(i, n):
                here, moved = started.pop((i, n))
                east_of = [jnp.where(last_lane, moved[(j + 1) % tiles], moved[j]) for j in range(tiles)]
                flux = [
                    a * x - b * y for a, b, x, y in zip(load(dx, (0, k), i), load(vx, (0, k), i), east_of, here)
                ]
                fluxes[i, n] = here, flux, [pltpu.roll(x, 1, 1) for x in flux]

            def north_flux(i, here, above):
                return [a * x - b * y for a, b, x, y in zip(load(dx, (1, k), i), load(vx, (1, k), i), above, here)]

            def finish(i, n):
                here, flux, moved = fluxes.pop((i, n))
                lifted = [pltpu.roll(x, 7, 0) for x in load(src, (n, k), i + 1)]
                above = [jnp.where(last_row, a, b) for a, b in zip(lifted, turned[i, n])]
                flux_n = north_flux(i, here, above)
                dropped = [pltpu.roll(x, 1, 0) for x in flux_n]
                higher = load(src, (n, k + 1), i)
                flux_v = [c * (x - y) for c, x, y in zip(load(dx, (2, k), i), higher, here)]
                flux_u = load(vbuf, (n,), i)
                rows = pl.ds(8 * i, 8)
                for j in range(tiles):
                    vbuf[n, rows, pl.ds(128 * j, 128)] = flux_v[j]
                    if last and j == tiles - 1:
                        continue
                    new = here[j] + (flux_n[j] - jnp.where(first_row, below[i, n][j], dropped[j]))
                    new = new + (flux[j] - jnp.where(first_lane, moved[j - 1], moved[j])) + (flux_v[j] - flux_u[j])
                    dst[n, k, rows, pl.ds(128 * j, 128)] = new
                turned[i + 1, n], below[i + 1, n] = lifted, dropped

            chunks = []
            for first, count in starts:
                for n in range(2):
                    prev = (first - 1) % STRIPS
                    tail, head = load(src, (n, k), prev), load(src, (n, k), first)
                    turned[first, n] = [pltpu.roll(x, 7, 0) for x in head]
                    above = [jnp.where(last_row, a, pltpu.roll(b, 7, 0)) for a, b in zip(turned[first, n], tail)]
                    below[first, n] = [pltpu.roll(x, 1, 0) for x in north_flux(prev, tail, above)]
                chunks += [(first + i, n) for i in range(count) for n in range(2)]
            for at in range(len(chunks) + 2 * GAP):
                for stage, work in enumerate((start, face, finish)):
                    if 0 <= at - stage * GAP < len(chunks):
                        work(*chunks[at - stage * GAP])

    for number, (src, dst) in enumerate(((c0, c1), (c1, c0), (c0, out_ref))):
        vbuf[...] = jnp.zeros((2, EH, EW), F32)
        sweep(src, dst, number == 2, [(1, 6)])
        for copy in rims[number]:
            copy.wait()
        sweep(src, dst, number == 2, [(7, 1), (0, 1)])
        if number < 2:
            exchange(dst, number + 1)

    plane = jnp.concatenate([out_ref[0, 0], out_ref[1, 0]], axis=0)
    nexts = pltpu.roll(plane, W - 1, 1)
    lhs = jnp.concatenate(list(split(plane)) + list(split(nexts)), axis=0)
    line = iota((H, 128), 0).astype(F32)
    for g in range(5):
        res = jnp.dot(lhs, hot[:, pl.ds(512 * g, 512)], preferred_element_type=F32)
        for s in range(4):
            part = res[:, 128 * s : 128 * s + 128]
            frac = fracs[4 * g + s]
            along = (1.0 - frac) * (part[0:128] + part[128:256]) + frac * (part[256:384] + part[384:512])
            ypos = blocks[g][s : s + 1, 384:512] * (H - 1.0)
            tent = jnp.maximum(0.0, 1.0 - jnp.abs(ypos - line))
            flag = blocks[g][s : s + 1, 512:640]
            for n in range(2):
                sample = jnp.sum(along[H * n : H * n + H] * tent, axis=0, keepdims=True)
                value = flag * (0.5 * blocks[g][s : s + 1, 128 * n : 128 * n + 128] + 0.5 * sample)
                if g in reach:
                    value = reach[g] * value
                fout_ref[4 * g + s, pl.ds(n, 1), :] = value


def shards(tracers, diffusivity, velocity, wet_mask, argo_rows, argo_dest, argo_cols, argo_count, float_values, float_pos, float_dest):
    vmem = pl.BlockSpec(memory_space=pltpu.VMEM)
    hbm = pl.BlockSpec(memory_space=pltpu.HBM)
    dma, scratch = pltpu.SemaphoreType.DMA, pltpu.VMEM
    return pl.pallas_call(
        kernel,
        out_shape=(
            pltpu.VMEM(tracers.shape, F32),
            pltpu.VMEM((20, 2, 128), F32),
        ),
        in_specs=[hbm] * 11,
        out_specs=(vmem, vmem),
        scratch_shapes=[
            scratch((2, LEVELS + 1, EH, EW), F32),
            scratch((2, LEVELS + 1, EH, EW), F32),
            scratch((3, LEVELS, EH, EW), F32),
            scratch((2, LEVELS, EH, EW), F32),
            scratch((LEVELS, EH, W), I32),
            scratch((LEVELS + 1, EH, EW), F32),
            scratch((2, EH, EW), F32),
            scratch((4, H, 128), F32),
            scratch((4, H, 128), F32),
            scratch((4, H, 128), F32),
            scratch((4, 8, 128), F32),
            scratch((4, 8, 128), F32),
            scratch((4, 8, 128), F32),
            scratch((4, 8, 128), F32),
            scratch((8, 4, 4, 1, 128), F32),
            scratch((8, 4, 4, 1, 128), F32),
            scratch((16, 8, 1, 128), F32),
            scratch((5, 8, 640), F32),
            scratch((4, 8, 640), F32),
            scratch((H * 21, 512), BF16),
            scratch((W, 2560), BF16),
            scratch((128, 512), BF16),
            scratch((128, 128), F32),
            scratch((1, 128), I32),
            scratch((1, 128), I32),
            pltpu.SMEM((1,), I32),
            scratch((16, 2, 128), F32),
            scratch((16, 2, 128), F32),
            scratch((1, 16), I32),
            dma((7,)), dma((4,)), dma, dma, dma, dma, dma((4,)), dma((4,)), dma((6,)), dma((6,)), dma((4,)), dma((4,)),
            dma((6,)), dma((6,)),
        ],
        compiler_params=pltpu.CompilerParams(
            collective_id=1, has_side_effects=True, vmem_limit_bytes=61 * 1024 * 1024
        ),
    )(
        tracers, diffusivity, velocity, wet_mask, argo_rows, argo_dest.reshape(1, -1), argo_cols.reshape(1, -1),
        argo_count, float_values, float_pos, float_dest.reshape(1, -1),
    )


def solution(mesh):
    grid4, grid3 = P(None, None, "lat", "lon"), P(None, "lat", "lon")
    tiles = ("lon", "lat")
    return jax.shard_map(
        shards,
        mesh=mesh,
        in_specs=(
            grid4, grid4, grid4, grid3, P(tiles, None), P(tiles, None), P(tiles), P(tiles),
            P(tiles, None, None), P(tiles, None, None), P(tiles, None),
        ),
        out_specs=(grid4, P(tiles, None, None)),
        check_vma=False,
    )
```

```python
import functools

import jax
import jax.numpy as jnp
from jax import lax
from jax.experimental import pallas as pl
from jax.experimental.pallas import tpu as pltpu
from jax.sharding import PartitionSpec as P

MESH = pl.DeviceIdType.MESH
F32, BF16, I32 = jnp.float32, jnp.bfloat16, jnp.int32

LEVELS, H, W = 10, 64, 512
EH, EW = 72, 640
STRIPS = EH // 8
GAP = 3
PAY = 21


def split(x):
    high = x.astype(BF16)
    return high, (x - high.astype(F32)).astype(BF16)


def iota(shape, dim):
    return lax.broadcasted_iota(I32, shape, dim)


def column_of(row):
    n = row.shape[1]
    wide = jnp.broadcast_to(row, (n, n))
    return jnp.sum(jnp.where(iota((n, n), 0) == iota((n, n), 1), wide, 0.0), axis=1, keepdims=True)


def ranks_of(row):
    n = row.shape[1]
    earlier = (column_of(row) == row) & (iota((n, n), 0) < iota((n, n), 1))
    return jnp.sum(earlier.astype(F32), axis=0, keepdims=True)


def places():
    lon, lat = lax.axis_index("lon"), lax.axis_index("lat")
    z, b = lon % 4, lon // 4
    u, v = (b % 2) * 4 + lat, (b // 2) * 4 + z
    return lon, lat, u, v


def device_of(u, v):
    return ((v // 4) * 8 + (u // 4) * 4 + v % 4, u % 4)


def kernel(
    tr_hbm, di_hbm, ve_hbm, wet_hbm, rows_hbm, dest_hbm, cols_hbm, count_hbm, fval_hbm, fpos_hbm, fdest_hbm,
    out_ref, fout_ref,
    c0, c1, dx, vx, wi, wf, vbuf, packs, from_w, from_e, from_nw, from_sw, from_ne, from_se,
    msg, mid, got, fsend, fgot, amat, hot, spread,
    rows_ref, dest_ref, cols_ref, count_ref, fval_ref, fpos_ref, fdest_ref,
    small_sem, load_sem, p1_s, p1_r, p2_s, p2_r, ns_s, ns_r, ew_s, ew_r, fl_s, fl_r, row_s, row_r,
):
    lon, lat, u, v = places()
    east, west = ((lon + 1) % 32, lat), ((lon + 31) % 32, lat)
    north, south = (lon, (lat + 1) % 4), (lon, (lat + 3) % 4)
    ne, se = (east[0], north[1]), (east[0], south[1])
    nw, sw = (west[0], north[1]), (west[0], south[1])
    barrier = pltpu.get_barrier_semaphore()

    smalls = [
        pltpu.make_async_copy(src, dst, small_sem.at[i])
        for i, (src, dst) in enumerate((
            (rows_hbm, rows_ref), (dest_hbm, dest_ref), (cols_hbm, cols_ref), (count_hbm, count_ref),
            (fval_hbm, fval_ref), (fpos_hbm, fpos_ref), (fdest_hbm, fdest_ref),
        ))
    ]
    for copy in smalls:
        copy.start()

    @pl.loop(1, 8)
    def _(d):
        pl.semaphore_signal(barrier, inc=1, device_id=device_of((u + d) % 8, v), device_id_type=MESH)

    @pl.loop(1, 16)
    def _(d):
        pl.semaphore_signal(barrier, inc=1, device_id=device_of(u, (v + d) % 16), device_id_type=MESH)

    for peer in (east, west, north, south, ne, se, nw, sw):
        pl.semaphore_signal(barrier, inc=1, device_id=peer, device_id_type=MESH)

    rows = pl.ds(0, H)
    loads = []
    for a, n in ((0, 128), (384, 128), (128, 256)):
        lanes = pl.ds(a, n)
        for src, dst in (
            (wet_hbm.at[:, :, lanes], wi.at[:, rows, lanes]),
            (di_hbm.at[:, :, :, lanes], dx.at[:, :, rows, lanes]),
            (ve_hbm.at[:, :, :, lanes], vx.at[:, :, rows, lanes]),
            (tr_hbm.at[:, :, :, lanes], c0.at[:, pl.ds(0, LEVELS), rows, lanes]),
        ):
            loads.append(pltpu.make_async_copy(src, dst, load_sem.at[len(loads)]))
    for copy in loads:
        copy.start()

    for copy in smalls:
        copy.wait()

    lane = iota((128, 128), 1)
    sub = iota((128, 128), 0)
    level = jnp.where(sub >= PAY, sub - PAY, sub)
    tracer = jnp.where(level >= LEVELS, 1, 0)
    level = level - tracer * LEVELS
    depth = lane - tracer * 64
    weight = jnp.maximum(0.0, 1.0 - jnp.abs(depth.astype(F32) * ((LEVELS - 1) / 63.0) - level.astype(F32)))
    weight = jnp.where((depth >= 0) & (depth < 64), weight, 0.0)
    total = jnp.sum(weight, axis=1, keepdims=True)
    table = 0.5 * weight / jnp.where(total > 0.0, total, 1.0)
    pay = lax.dot_general(
        table, rows_ref[...], (((1,), (1,)), ((), ())), precision=lax.Precision.HIGHEST, preferred_element_type=F32
    )
    cell = (cols_ref[...] + 1).astype(F32)
    pay = jnp.where((sub == PAY - 1) | (sub == 2 * PAY - 1), jnp.broadcast_to(cell, (128, 128)), pay)
    pay = jnp.concatenate([jnp.where(sub < PAY, pay, 0.0), jnp.where((sub >= PAY) & (sub < 2 * PAY), pay, 0.0)], axis=1)
    live = iota((1, 128), 1) < count_ref[0]
    dest = jnp.where(live, dest_ref[...], -5).astype(F32)
    rank = ranks_of(dest)
    tile = ((sub % 32) * 4 + sub // 32).astype(F32)
    first = jnp.where((tile == dest) & (rank == 0.0), 1.0, 0.0)
    second = jnp.where((tile == dest) & (rank == 1.0), 1.0, 0.0)
    chosen = jnp.concatenate([first, second], axis=1).astype(BF16)
    ordered = sum(
        lax.dot_general(chosen, part, (((1,), (1,)), ((), ())), preferred_element_type=F32) for part in split(pay)
    )
    for b in range(4):
        mine = ordered[32 * b : 32 * b + 32]
        full = pltpu.roll(mine, 1, 0) + pltpu.roll(mine, 2 * PAY, 1) + pltpu.roll(pltpu.roll(mine, 31, 0), 4 * PAY, 1)
        for h in range(2):
            for y in range(4):
                for z in range(4):
                    at = 8 * y + 4 * h + z
                    msg[4 * h + b, y, z] = full[at : at + 1]

    fdest = fdest_ref[...].astype(F32)
    place = 8.0 * fdest + ranks_of(fdest)
    fhot = (iota((40, 16), 0).astype(F32) == place).astype(F32)
    fpay = jnp.concatenate([fval_ref[:, 0], fval_ref[:, 1], fpos_ref[:, 0], fpos_ref[:, 1]], axis=1)
    fordered = jnp.dot(fhot, fpay, precision=lax.Precision.HIGHEST, preferred_element_type=F32)
    fsend[:, :, pl.ds(0, 512)] = fordered.reshape(5, 8, 512)
    flags = jnp.broadcast_to(jnp.sum(fhot, axis=1, keepdims=True), (40, 128))
    fsend[:, :, pl.ds(512, 128)] = flags.reshape(5, 8, 128)

    pl.semaphore_wait(barrier, 30)

    def remote(src, dst, s, r, peer):
        return pltpu.make_async_remote_copy(
            src_ref=src, dst_ref=dst, send_sem=s, recv_sem=r, device_id=peer, device_id_type=MESH
        )

    @pl.loop(1, 8)
    def _(d):
        t = (u + d) % 8
        remote(msg.at[t], mid.at[d], p1_s, p1_r, device_of(t, v)).start()

    top, bottom = pl.ds(H - 1, 1), pl.ds(0, 1)
    low, high = pl.ds(EH - 1, 1), pl.ds(H, 1)
    wide = pl.ds(0, W)
    edge = [
        remote(di_hbm.at[1, :, top], dx.at[1, :, low, wide], ns_s.at[0], ns_r.at[0], north),
        remote(ve_hbm.at[1, :, top], vx.at[1, :, low, wide], ns_s.at[1], ns_r.at[1], north),
        remote(wet_hbm.at[:, top], wi.at[:, low], ns_s.at[2], ns_r.at[2], north),
        remote(wet_hbm.at[:, bottom], wi.at[:, high], ns_s.at[3], ns_r.at[3], south),
    ]
    for i, peer in enumerate((east, west, north, south)):
        edge.append(remote(fsend.at[1 + i], fgot.at[i], fl_s.at[i], fl_r.at[i], peer))
    for copy in edge:
        copy.start()
    mid[0] = msg[u]

    for copy in loads[:8]:
        copy.wait()

    lane64 = iota((H, 128), 1)

    def planes_of(t):
        for q in range(20):
            n, k = q // LEVELS, q % LEVELS
            yield q, ((c0, (n, k)), (dx, (0, k)) if n == 0 else (vx, (0, k)), (dx, (1, k)) if n == 0 else (vx, (1, k)), (dx, (2, k)) if n == 0 else (wf, (k,)))[t]

    for k in range(LEVELS):
        for a in (0, 384):
            wf[k, rows, pl.ds(a, 128)] = wi[k, rows, pl.ds(a, 128)].astype(F32)
    for t in range(4):
        acc = jnp.zeros((H, 128), F32)
        for q, (ref, at) in planes_of(t):
            left = ref[at + (pl.ds(0, H), pl.ds(0, 128))]
            right = ref[at + (pl.ds(0, H), pl.ds(384, 128))]
            both = pltpu.roll(jnp.where(lane64 < 3, left, right), 6 * q + 3, 1)
            acc = jnp.where(lane64 >= 6 * q, both, acc)
        packs[t] = acc
    sides = [
        remote(packs, from_w, ew_s.at[0], ew_r.at[0], east),
        remote(packs, from_e, ew_s.at[1], ew_r.at[1], west),
        remote(packs.at[:, pl.ds(56, 8)], from_sw, ew_s.at[2], ew_r.at[2], ne),
        remote(packs.at[:, pl.ds(56, 8)], from_se, ew_s.at[3], ew_r.at[3], nw),
        remote(packs.at[:, pl.ds(0, 8)], from_nw, ew_s.at[4], ew_r.at[4], se),
        remote(packs.at[:, pl.ds(0, 8)], from_ne, ew_s.at[5], ew_r.at[5], sw),
    ]
    for copy in sides:
        copy.start()

    done = remote(mid.at[pl.ds(1, 7)], mid.at[pl.ds(1, 7)], p1_s, p1_r, east)
    done.wait_send()
    done.wait_recv()

    @pl.loop(1, 16)
    def _(d):
        t = (v + d) % 16
        remote(mid.at[:, t // 4, t % 4], got.at[d], p2_s, p2_r, device_of(u, t)).start()

    got[0] = mid[:, v // 4, v % 4]

    for copy in loads[8:]:
        copy.wait()
    for k in range(LEVELS):
        wf[k, rows, pl.ds(128, 256)] = wi[k, rows, pl.ds(128, 256)].astype(F32)

    sub8 = iota((8, EW), 0)

    def up(cur, nxt):
        n = cur.shape[1]
        return jnp.where(sub8[:, :n] == 7, pltpu.roll(nxt, 7, 0), pltpu.roll(cur, 7, 0))

    def coefficients(k, strip, a, b):
        rows = pl.ds(8 * strip, 8)
        after = pl.ds(8 * ((strip + 1) % STRIPS), 8)
        lanes = pl.ds(a, b - a)
        w = wf[k, rows, lanes]
        if b < EW:
            w_e = pltpu.roll(wf[k, rows, pl.ds(a, b - a + 128)], b - a + 127, 1)[:, : b - a]
        elif a == 0:
            w_e = pltpu.roll(w, EW - 1, 1)
        else:
            w_e = jnp.concatenate([w, wf[k, rows, pl.ds(0, 128)]], axis=1)
            w_e = pltpu.roll(w_e, b - a + 127, 1)[:, : b - a]
        w_n = up(w, wf[k, after, lanes])
        w_v = wf[k + 1, rows, lanes]
        for i, other in ((0, w_e), (1, w_n)):
            if strip == 8 and i == 0:
                continue
            d, f, open_ = dx[i, k, rows, lanes], 0.5 * vx[i, k, rows, lanes], w * other
            dx[i, k, rows, lanes] = open_ * (d - f)
            vx[i, k, rows, lanes] = open_ * (d + f)
        if strip < 8:
            dx[2, k, rows, lanes] = w * w_v * dx[2, k, rows, lanes]

    wf[LEVELS] = jnp.zeros((EH, EW), F32)
    for n in range(2):
        c0[n, LEVELS] = jnp.zeros((EH, EW), F32)
        c1[n, LEVELS] = jnp.zeros((EH, EW), F32)

    @pl.loop(0, LEVELS)
    def _(k):
        for strip in range(7):
            coefficients(k, strip, 0, 384)

    spread_lane = iota((128, 128), 1)
    within = spread_lane % 6
    picked = spread_lane // 6
    inner = spread_lane < 120
    for b, start in enumerate((0, PAY, 4 * PAY, 5 * PAY)):
        hit = (iota((128, 128), 0) == start + picked) & inner
        spread[:, pl.ds(128 * b, 128)] = jnp.where(hit, 1.0, 0.0).astype(BF16)
    targets = (
        jnp.where((within < 3) & inner, 509 + within, -1), jnp.where((within >= 3) & inner, within - 3, -1)
    )

    for i in range(4):
        edge[4 + i].wait()
    blocks = [fsend[0]] + [fgot[i] for i in range(4)]
    reach = {3: jnp.where(lat > 0, 1.0, 0.0), 4: jnp.where(lat < 3, 1.0, 0.0)}
    cells = iota((W, 128), 0)
    lows, fracs = [], []
    for g in range(5):
        for s in range(4):
            xpos = blocks[g][s : s + 1, 256:384] * (W - 1.0)
            lowest = jnp.clip(jnp.floor(xpos).astype(I32), 0, W - 2)
            fracs.append(xpos - lowest.astype(F32))
            hot[:, pl.ds(512 * g + 128 * s, 128)] = jnp.where(cells == lowest, 1.0, 0.0).astype(BF16)

    for copy in edge[:4] + sides:
        copy.wait()
    inside = jnp.where(iota((8, W), 0) < 4, jnp.where(lat < 3, 1, 0), jnp.where(lat > 0, 1, 0))
    for k in range(LEVELS):
        wf[k, pl.ds(H, 8), wide] = jnp.where(inside > 0, wi[k, pl.ds(H, 8)].astype(F32), 0.0)
    lane8 = iota((8, 128), 1)
    side = []
    for t in range(4):
        body = jnp.where(lane64 % 6 < 3, from_w[t], from_e[t])
        upper = jnp.where(lane8 % 6 < 3, from_nw[t], from_ne[t])
        lower = jnp.where(lane8 % 6 < 3, from_sw[t], from_se[t])
        side.append(jnp.concatenate([body, jnp.where(sub8[:, :128] < 4, upper, lower)], axis=0))

    def unpack(t, q, ref, at):
        values = pltpu.roll(side[t], (128 - 6 * q - 3) % 128, 1)
        if ref is wf:
            edge_rows = jnp.where(inside[:, :128] > 0, values[H:], 0.0)
            values = jnp.concatenate([values[:H], edge_rows], axis=0)
        return ref, at, values

    def unpack_all(blocks_of):
        held = []
        for t in blocks_of:
            for q, (ref, at) in planes_of(t):
                held.append(unpack(t, q, ref, at))
                if len(held) > 3:
                    ref, at, values = held.pop(0)
                    ref[at + (pl.ds(0, values.shape[0]), pl.ds(W, 128))] = values
        for ref, at, values in held:
            ref[at + (pl.ds(0, values.shape[0]), pl.ds(W, 128))] = values

    unpack_all((1, 2, 3))

    @pl.loop(0, LEVELS)
    def _(k):
        for strip in range(7):
            coefficients(k, strip, 384, EW)
        coefficients(k, 7, 0, EW)
        coefficients(k, 8, 0, EW)

    done = remote(got.at[pl.ds(1, 15)], got.at[pl.ds(1, 15)], p2_s, p2_r, east)
    done.wait_send()
    done.wait_recv()

    rims = {}

    def exchange(ref, number):
        def rim(a, b, i, peer):
            at = [ref.at[:, pl.ds(0, LEVELS), pl.ds(r, 1)] for r in (a, b)]
            return remote(at[0], at[1], row_s.at[2 * number + i], row_r.at[2 * number + i], peer)

        rims[number] = rim(H - 1, EH - 1, 0, north), rim(0, H, 1, south)
        for copy in rims[number]:
            copy.start()

    vals = got[...].reshape(128, 128)
    valsT = vals.T
    cols = (vals.astype(I32) - 1) & (W - 1)
    rowsT = (valsT.astype(I32) - 1) >> 9

    grown = [jnp.dot(part, spread[...], preferred_element_type=F32) for part in split(vals)]
    sub64 = iota((H, 128), 0)
    pick, hi_parts, lo_parts, ones = [], [], [], []
    for b, start in enumerate((0, PAY, 4 * PAY, 5 * PAY)):
        at = start + PAY - 1
        pick.append(jnp.where(sub64 == rowsT[at : at + 1], 1.0, 0.0))
        match = jnp.where(cols[:, at : at + 1] == targets[b // 2], 1.0, 0.0)
        hi_parts.append(match * grown[0][:, 128 * b : 128 * b + 128])
        lo_parts.append(match * grown[1][:, 128 * b : 128 * b + 128])
        ones.append(match)
    pick = jnp.concatenate(pick, axis=1).astype(BF16)
    onto = jnp.concatenate([jnp.concatenate(p, axis=0).astype(BF16) for p in (hi_parts, lo_parts, ones)], axis=1)
    beside = jnp.dot(pick, onto, preferred_element_type=F32)

    wide_lane = iota((128, W), 1)
    slots = (2 * PAY, 3 * PAY)
    own_rows = jnp.concatenate([rowsT[b + PAY - 1 : b + PAY] for b in slots], axis=1)
    own = jnp.where(iota((H, 256), 0) == own_rows, 1.0, 0.0)
    for c in range(20):
        value = jnp.concatenate([valsT[b + c : b + c + 1] for b in slots], axis=1)
        value_hi = value.astype(BF16).astype(F32)
        amat[pl.ds(H * c, H), pl.ds(0, 256)] = (own * value_hi).astype(BF16)
        amat[pl.ds(H * c, H), pl.ds(256, 256)] = (own * (value - value_hi)).astype(BF16)
    amat[pl.ds(H * 20, H), pl.ds(0, 256)] = own.astype(BF16)
    amat[pl.ds(H * 20, H), pl.ds(256, 256)] = jnp.zeros((H, 256), BF16)
    onto = [jnp.where(wide_lane == cols[:, b + PAY - 1 : b + PAY], 1.0, 0.0) for b in slots]
    onto = jnp.concatenate(onto + onto, axis=0).astype(BF16)
    added = jnp.dot(amat[...], onto, preferred_element_type=F32)
    keep = 1.0 - 0.5 * added[H * 20 :]
    for c in range(20):
        at = (c // LEVELS, c % LEVELS, pl.ds(0, H), wide)
        c0[at] = c0[at] * keep + added[H * c : H * c + H]
    body = side[0][:H]
    side[0] = body * (1.0 - 0.5 * beside[:, 256:384]) + beside[:, 0:128] + beside[:, 128:256]

    unpack_all((0,))
    exchange(c0, 0)

    tiles = EW // 128
    first_lane, last_lane = iota((8, 128), 1) == 0, iota((8, 128), 1) == 127
    first_row, last_row = iota((8, 128), 0) == 0, iota((8, 128), 0) == 7

    def sweep(src, dst, last, starts):
        @pl.loop(0, LEVELS)
        def _(k):
            def load(ref, at, i):
                return [ref[at + (pl.ds(8 * (i % STRIPS), 8), pl.ds(128 * j, 128))] for j in range(tiles)]

            started, fluxes, turned, below = {}, {}, {}, {}

            def start(i, n):
                here = load(src, (n, k), i)
                started[i, n] = here, [pltpu.roll(x, 127, 1) for x in here]

            def face(i, n):
                here, moved = started.pop((i, n))
                east_of = [jnp.where(last_lane, moved[(j + 1) % tiles], moved[j]) for j in range(tiles)]
                flux = [
                    a * x - b * y for a, b, x, y in zip(load(dx, (0, k), i), load(vx, (0, k), i), east_of, here)
                ]
                fluxes[i, n] = here, flux, [pltpu.roll(x, 1, 1) for x in flux]

            def north_flux(i, here, above):
                return [a * x - b * y for a, b, x, y in zip(load(dx, (1, k), i), load(vx, (1, k), i), above, here)]

            def finish(i, n):
                here, flux, moved = fluxes.pop((i, n))
                lifted = [pltpu.roll(x, 7, 0) for x in load(src, (n, k), i + 1)]
                above = [jnp.where(last_row, a, b) for a, b in zip(lifted, turned[i, n])]
                flux_n = north_flux(i, here, above)
                dropped = [pltpu.roll(x, 1, 0) for x in flux_n]
                higher = load(src, (n, k + 1), i)
                flux_v = [c * (x - y) for c, x, y in zip(load(dx, (2, k), i), higher, here)]
                flux_u = load(vbuf, (n,), i)
                rows = pl.ds(8 * i, 8)
                for j in range(tiles):
                    vbuf[n, rows, pl.ds(128 * j, 128)] = flux_v[j]
                    if last and j == tiles - 1:
                        continue
                    new = here[j] + (flux_n[j] - jnp.where(first_row, below[i, n][j], dropped[j]))
                    new = new + (flux[j] - jnp.where(first_lane, moved[j - 1], moved[j])) + (flux_v[j] - flux_u[j])
                    dst[n, k, rows, pl.ds(128 * j, 128)] = new
                turned[i + 1, n], below[i + 1, n] = lifted, dropped

            chunks = []
            for first, count in starts:
                for n in range(2):
                    prev = (first - 1) % STRIPS
                    tail, head = load(src, (n, k), prev), load(src, (n, k), first)
                    turned[first, n] = [pltpu.roll(x, 7, 0) for x in head]
                    above = [jnp.where(last_row, a, pltpu.roll(b, 7, 0)) for a, b in zip(turned[first, n], tail)]
                    below[first, n] = [pltpu.roll(x, 1, 0) for x in north_flux(prev, tail, above)]
                chunks += [(first + i, n) for i in range(count) for n in range(2)]
            for at in range(len(chunks) + 2 * GAP):
                for stage, work in enumerate((start, face, finish)):
                    if 0 <= at - stage * GAP < len(chunks):
                        work(*chunks[at - stage * GAP])

    for number, (src, dst) in enumerate(((c0, c1), (c1, c0), (c0, out_ref))):
        vbuf[...] = jnp.zeros((2, EH, EW), F32)
        sweep(src, dst, number == 2, [(1, 6)])
        for copy in rims[number]:
            copy.wait()
        sweep(src, dst, number == 2, [(7, 1), (0, 1)])
        if number < 2:
            exchange(dst, number + 1)

    plane = jnp.concatenate([out_ref[0, 0], out_ref[1, 0]], axis=0)
    nexts = pltpu.roll(plane, W - 1, 1)
    lhs = jnp.concatenate(list(split(plane)) + list(split(nexts)), axis=0)
    line = iota((H, 128), 0).astype(F32)
    for g in range(5):
        res = jnp.dot(lhs, hot[:, pl.ds(512 * g, 512)], preferred_element_type=F32)
        for s in range(4):
            part = res[:, 128 * s : 128 * s + 128]
            frac = fracs[4 * g + s]
            along = (1.0 - frac) * (part[0:128] + part[128:256]) + frac * (part[256:384] + part[384:512])
            ypos = blocks[g][s : s + 1, 384:512] * (H - 1.0)
            tent = jnp.maximum(0.0, 1.0 - jnp.abs(ypos - line))
            flag = blocks[g][s : s + 1, 512:640]
            for n in range(2):
                sample = jnp.sum(along[H * n : H * n + H] * tent, axis=0, keepdims=True)
                value = flag * (0.5 * blocks[g][s : s + 1, 128 * n : 128 * n + 128] + 0.5 * sample)
                if g in reach:
                    value = reach[g] * value
                fout_ref[4 * g + s, pl.ds(n, 1), :] = value


def shards(tracers, diffusivity, velocity, wet_mask, argo_rows, argo_dest, argo_cols, argo_count, float_values, float_pos, float_dest):
    vmem = pl.BlockSpec(memory_space=pltpu.VMEM)
    hbm = pl.BlockSpec(memory_space=pltpu.HBM)
    dma, scratch = pltpu.SemaphoreType.DMA, pltpu.VMEM
    return pl.pallas_call(
        kernel,
        out_shape=(
            pltpu.VMEM(tracers.shape, F32),
            pltpu.VMEM((20, 2, 128), F32),
        ),
        in_specs=[hbm] * 11,
        out_specs=(vmem, vmem),
        scratch_shapes=[
            scratch((2, LEVELS + 1, EH, EW), F32),
            scratch((2, LEVELS + 1, EH, EW), F32),
            scratch((3, LEVELS, EH, EW), F32),
            scratch((2, LEVELS, EH, EW), F32),
            scratch((LEVELS, EH, W), I32),
            scratch((LEVELS + 1, EH, EW), F32),
            scratch((2, EH, EW), F32),
            scratch((4, H, 128), F32),
            scratch((4, H, 128), F32),
            scratch((4, H, 128), F32),
            scratch((4, 8, 128), F32),
            scratch((4, 8, 128), F32),
            scratch((4, 8, 128), F32),
            scratch((4, 8, 128), F32),
            scratch((8, 4, 4, 1, 128), F32),
            scratch((8, 4, 4, 1, 128), F32),
            scratch((16, 8, 1, 128), F32),
            scratch((5, 8, 640), F32),
            scratch((4, 8, 640), F32),
            scratch((H * 21, 512), BF16),
            scratch((W, 2560), BF16),
            scratch((128, 512), BF16),
            scratch((128, 128), F32),
            scratch((1, 128), I32),
            scratch((1, 128), I32),
            pltpu.SMEM((1,), I32),
            scratch((16, 2, 128), F32),
            scratch((16, 2, 128), F32),
            scratch((1, 16), I32),
            dma((7,)), dma((12,)), dma, dma, dma, dma, dma((4,)), dma((4,)), dma((6,)), dma((6,)), dma((4,)), dma((4,)),
            dma((6,)), dma((6,)),
        ],
        compiler_params=pltpu.CompilerParams(
            collective_id=1, has_side_effects=True, vmem_limit_bytes=61 * 1024 * 1024
        ),
    )(
        tracers, diffusivity, velocity, wet_mask, argo_rows, argo_dest.reshape(1, -1), argo_cols.reshape(1, -1),
        argo_count, float_values, float_pos, float_dest.reshape(1, -1),
    )


def solution(mesh):
    grid4, grid3 = P(None, None, "lat", "lon"), P(None, "lat", "lon")
    tiles = ("lon", "lat")
    return jax.shard_map(
        shards,
        mesh=mesh,
        in_specs=(
            grid4, grid4, grid4, grid3, P(tiles, None), P(tiles, None), P(tiles), P(tiles),
            P(tiles, None, None), P(tiles, None, None), P(tiles, None),
        ),
        out_specs=(grid4, P(tiles, None, None)),
        check_vma=False,
    )
```

```python
import functools

import jax
import jax.numpy as jnp
from jax import lax
from jax.experimental import pallas as pl
from jax.experimental.pallas import tpu as pltpu
from jax.sharding import PartitionSpec as P

MESH = pl.DeviceIdType.MESH
F32, BF16, I32 = jnp.float32, jnp.bfloat16, jnp.int32

LEVELS, H, W = 10, 64, 512
EH, EW = 72, 640
STRIPS = EH // 8
GAP = 3
PAY = 21


def split(x):
    high = x.astype(BF16)
    return high, (x - high.astype(F32)).astype(BF16)


def iota(shape, dim):
    return lax.broadcasted_iota(I32, shape, dim)


def column_of(row):
    n = row.shape[1]
    wide = jnp.broadcast_to(row, (n, n))
    return jnp.sum(jnp.where(iota((n, n), 0) == iota((n, n), 1), wide, 0.0), axis=1, keepdims=True)


def ranks_of(row):
    n = row.shape[1]
    earlier = (column_of(row) == row) & (iota((n, n), 0) < iota((n, n), 1))
    return jnp.sum(earlier.astype(F32), axis=0, keepdims=True)


def places():
    lon, lat = lax.axis_index("lon"), lax.axis_index("lat")
    z, b = lon % 4, lon // 4
    u, v = (b % 2) * 4 + lat, (b // 2) * 4 + z
    return lon, lat, u, v


def device_of(u, v):
    return ((v // 4) * 8 + (u // 4) * 4 + v % 4, u % 4)


def kernel(
    tr_hbm, di_hbm, ve_hbm, wet_hbm, rows_hbm, dest_hbm, cols_hbm, count_hbm, fval_hbm, fpos_hbm, fdest_hbm,
    out_ref, fout_ref,
    c0, c1, dx, vx, wi, wf, vbuf, packs, from_w, from_e, from_nw, from_sw, from_ne, from_se,
    msg, mid, got, fsend, fgot, amat, hot, spread,
    rows_ref, dest_ref, cols_ref, count_ref, fval_ref, fpos_ref, fdest_ref,
    small_sem, load_sem, p1_s, p1_r, p2_s, p2_r, ns_s, ns_r, ew_s, ew_r, fl_s, fl_r, row_s, row_r,
):
    lon, lat, u, v = places()
    east, west = ((lon + 1) % 32, lat), ((lon + 31) % 32, lat)
    north, south = (lon, (lat + 1) % 4), (lon, (lat + 3) % 4)
    ne, se = (east[0], north[1]), (east[0], south[1])
    nw, sw = (west[0], north[1]), (west[0], south[1])
    barrier = pltpu.get_barrier_semaphore()

    smalls = [
        pltpu.make_async_copy(src, dst, small_sem.at[i])
        for i, (src, dst) in enumerate((
            (rows_hbm, rows_ref), (dest_hbm, dest_ref), (cols_hbm, cols_ref), (count_hbm, count_ref),
            (fval_hbm, fval_ref), (fpos_hbm, fpos_ref), (fdest_hbm, fdest_ref),
        ))
    ]
    for copy in smalls:
        copy.start()

    @pl.loop(1, 8)
    def _(d):
        pl.semaphore_signal(barrier, inc=1, device_id=device_of((u + d) % 8, v), device_id_type=MESH)

    @pl.loop(1, 16)
    def _(d):
        pl.semaphore_signal(barrier, inc=1, device_id=device_of(u, (v + d) % 16), device_id_type=MESH)

    for peer in (east, west, north, south, ne, se, nw, sw):
        pl.semaphore_signal(barrier, inc=1, device_id=peer, device_id_type=MESH)

    rows = pl.ds(0, H)
    loads = []
    for a, n in ((0, 128), (384, 128), (128, 256)):
        lanes = pl.ds(a, n)
        for src, dst in (
            (wet_hbm.at[:, :, lanes], wi.at[:, rows, lanes]),
            (di_hbm.at[:, :, :, lanes], dx.at[:, :, rows, lanes]),
            (ve_hbm.at[:, :, :, lanes], vx.at[:, :, rows, lanes]),
            (tr_hbm.at[:, :, :, lanes], c0.at[:, pl.ds(0, LEVELS), rows, lanes]),
        ):
            loads.append(pltpu.make_async_copy(src, dst, load_sem.at[len(loads)]))
    for copy in loads:
        copy.start()

    for copy in smalls:
        copy.wait()

    lane = iota((128, 128), 1)
    sub = iota((128, 128), 0)
    level = jnp.where(sub >= PAY, sub - PAY, sub)
    tracer = jnp.where(level >= LEVELS, 1, 0)
    level = level - tracer * LEVELS
    depth = lane - tracer * 64
    weight = jnp.maximum(0.0, 1.0 - jnp.abs(depth.astype(F32) * ((LEVELS - 1) / 63.0) - level.astype(F32)))
    weight = jnp.where((depth >= 0) & (depth < 64), weight, 0.0)
    total = jnp.sum(weight, axis=1, keepdims=True)
    table = 0.5 * weight / jnp.where(total > 0.0, total, 1.0)
    pay = lax.dot_general(
        table, rows_ref[...], (((1,), (1,)), ((), ())), precision=lax.Precision.HIGHEST, preferred_element_type=F32
    )
    cell = (cols_ref[...] + 1).astype(F32)
    pay = jnp.where((sub == PAY - 1) | (sub == 2 * PAY - 1), jnp.broadcast_to(cell, (128, 128)), pay)
    pay = jnp.concatenate([jnp.where(sub < PAY, pay, 0.0), jnp.where((sub >= PAY) & (sub < 2 * PAY), pay, 0.0)], axis=1)
    live = iota((1, 128), 1) < count_ref[0]
    dest = jnp.where(live, dest_ref[...], -5).astype(F32)
    rank = ranks_of(dest)
    tile = ((sub % 32) * 4 + sub // 32).astype(F32)
    first = jnp.where((tile == dest) & (rank == 0.0), 1.0, 0.0)
    second = jnp.where((tile == dest) & (rank == 1.0), 1.0, 0.0)
    chosen = jnp.concatenate([first, second], axis=1).astype(BF16)
    ordered = sum(
        lax.dot_general(chosen, part, (((1,), (1,)), ((), ())), preferred_element_type=F32) for part in split(pay)
    )
    for b in range(4):
        mine = ordered[32 * b : 32 * b + 32]
        full = pltpu.roll(mine, 1, 0) + pltpu.roll(mine, 2 * PAY, 1) + pltpu.roll(pltpu.roll(mine, 31, 0), 4 * PAY, 1)
        for h in range(2):
            for y in range(4):
                for z in range(4):
                    at = 8 * y + 4 * h + z
                    msg[4 * h + b, y, z] = full[at : at + 1]

    fdest = fdest_ref[...].astype(F32)
    place = 8.0 * fdest + ranks_of(fdest)
    fhot = (iota((40, 16), 0).astype(F32) == place).astype(F32)
    fpay = jnp.concatenate([fval_ref[:, 0], fval_ref[:, 1], fpos_ref[:, 0], fpos_ref[:, 1]], axis=1)
    fordered = jnp.dot(fhot, fpay, precision=lax.Precision.HIGHEST, preferred_element_type=F32)
    fsend[:, :, pl.ds(0, 512)] = fordered.reshape(5, 8, 512)
    flags = jnp.broadcast_to(jnp.sum(fhot, axis=1, keepdims=True), (40, 128))
    fsend[:, :, pl.ds(512, 128)] = flags.reshape(5, 8, 128)

    pl.semaphore_wait(barrier, 30)

    def remote(src, dst, s, r, peer):
        return pltpu.make_async_remote_copy(
            src_ref=src, dst_ref=dst, send_sem=s, recv_sem=r, device_id=peer, device_id_type=MESH
        )

    @pl.loop(1, 8)
    def _(d):
        t = (u + d) % 8
        remote(msg.at[t], mid.at[d], p1_s, p1_r, device_of(t, v)).start()

    top, bottom = pl.ds(H - 1, 1), pl.ds(0, 1)
    low, high = pl.ds(EH - 1, 1), pl.ds(H, 1)
    wide = pl.ds(0, W)
    edge = [
        remote(di_hbm.at[1, :, top], dx.at[1, :, low, wide], ns_s.at[0], ns_r.at[0], north),
        remote(ve_hbm.at[1, :, top], vx.at[1, :, low, wide], ns_s.at[1], ns_r.at[1], north),
        remote(wet_hbm.at[:, top], wi.at[:, low], ns_s.at[2], ns_r.at[2], north),
        remote(wet_hbm.at[:, bottom], wi.at[:, high], ns_s.at[3], ns_r.at[3], south),
    ]
    for i, peer in enumerate((east, west, north, south)):
        edge.append(remote(fsend.at[1 + i], fgot.at[i], fl_s.at[i], fl_r.at[i], peer))
    for copy in edge:
        copy.start()
    mid[0] = msg[u]

    for copy in loads[:8]:
        copy.wait()

    lane64 = iota((H, 128), 1)

    def planes_of(t):
        for q in range(20):
            n, k = q // LEVELS, q % LEVELS
            yield q, ((c0, (n, k)), (dx, (0, k)) if n == 0 else (vx, (0, k)), (dx, (1, k)) if n == 0 else (vx, (1, k)), (dx, (2, k)) if n == 0 else (wf, (k,)))[t]

    for k in range(LEVELS):
        for a in (0, 384):
            wf[k, rows, pl.ds(a, 128)] = wi[k, rows, pl.ds(a, 128)].astype(F32)
    for t in range(4):
        acc = jnp.zeros((H, 128), F32)
        for q, (ref, at) in planes_of(t):
            left = ref[at + (pl.ds(0, H), pl.ds(0, 128))]
            right = ref[at + (pl.ds(0, H), pl.ds(384, 128))]
            both = pltpu.roll(jnp.where(lane64 < 3, left, right), 6 * q + 3, 1)
            acc = jnp.where(lane64 >= 6 * q, both, acc)
        packs[t] = acc
    sides = [
        remote(packs, from_w, ew_s.at[0], ew_r.at[0], east),
        remote(packs, from_e, ew_s.at[1], ew_r.at[1], west),
        remote(packs.at[:, pl.ds(56, 8)], from_sw, ew_s.at[2], ew_r.at[2], ne),
        remote(packs.at[:, pl.ds(56, 8)], from_se, ew_s.at[3], ew_r.at[3], nw),
        remote(packs.at[:, pl.ds(0, 8)], from_nw, ew_s.at[4], ew_r.at[4], se),
        remote(packs.at[:, pl.ds(0, 8)], from_ne, ew_s.at[5], ew_r.at[5], sw),
    ]
    for copy in sides:
        copy.start()

    done = remote(mid.at[pl.ds(1, 7)], mid.at[pl.ds(1, 7)], p1_s, p1_r, east)
    done.wait_send()
    done.wait_recv()

    @pl.loop(1, 16)
    def _(d):
        t = (v + d) % 16
        remote(mid.at[:, t // 4, t % 4], got.at[d], p2_s, p2_r, device_of(u, t)).start()

    got[0] = mid[:, v // 4, v % 4]

    for copy in loads[8:]:
        copy.wait()
    for k in range(LEVELS):
        wf[k, rows, pl.ds(128, 256)] = wi[k, rows, pl.ds(128, 256)].astype(F32)

    sub8 = iota((8, EW), 0)

    def up(cur, nxt):
        n = cur.shape[1]
        return jnp.where(sub8[:, :n] == 7, pltpu.roll(nxt, 7, 0), pltpu.roll(cur, 7, 0))

    def coefficients(k, strip, a, b):
        rows = pl.ds(8 * strip, 8)
        after = pl.ds(8 * ((strip + 1) % STRIPS), 8)
        lanes = pl.ds(a, b - a)
        w = wf[k, rows, lanes]
        if b < EW:
            w_e = pltpu.roll(wf[k, rows, pl.ds(a, b - a + 128)], b - a + 127, 1)[:, : b - a]
        elif a == 0:
            w_e = pltpu.roll(w, EW - 1, 1)
        else:
            w_e = jnp.concatenate([w, wf[k, rows, pl.ds(0, 128)]], axis=1)
            w_e = pltpu.roll(w_e, b - a + 127, 1)[:, : b - a]
        w_n = up(w, wf[k, after, lanes])
        w_v = wf[k + 1, rows, lanes]
        for i, other in ((0, w_e), (1, w_n)):
            if strip == 8 and i == 0:
                continue
            d, f, open_ = dx[i, k, rows, lanes], 0.5 * vx[i, k, rows, lanes], w * other
            dx[i, k, rows, lanes] = open_ * (d - f)
            vx[i, k, rows, lanes] = open_ * (d + f)
        if strip < 8:
            dx[2, k, rows, lanes] = w * w_v * dx[2, k, rows, lanes]

    wf[LEVELS] = jnp.zeros((EH, EW), F32)
    for n in range(2):
        c0[n, LEVELS] = jnp.zeros((EH, EW), F32)
        c1[n, LEVELS] = jnp.zeros((EH, EW), F32)

    @pl.loop(0, LEVELS)
    def _(k):
        for strip in range(7):
            coefficients(k, strip, 0, 384)

    spread_lane = iota((128, 128), 1)
    within = spread_lane % 6
    picked = spread_lane // 6
    inner = spread_lane < 120
    for b, start in enumerate((0, PAY, 4 * PAY, 5 * PAY)):
        hit = (iota((128, 128), 0) == start + picked) & inner
        spread[:, pl.ds(128 * b, 128)] = jnp.where(hit, 1.0, 0.0).astype(BF16)
    targets = (
        jnp.where((within < 3) & inner, 509 + within, -1), jnp.where((within >= 3) & inner, within - 3, -1)
    )

    for i in range(4):
        edge[4 + i].wait()
    blocks = [fsend[0]] + [fgot[i] for i in range(4)]
    reach = {3: jnp.where(lat > 0, 1.0, 0.0), 4: jnp.where(lat < 3, 1.0, 0.0)}
    cells = iota((W, 128), 0)
    lows, fracs = [], []
    for g in range(5):
        for s in range(4):
            xpos = blocks[g][s : s + 1, 256:384] * (W - 1.0)
            lowest = jnp.clip(jnp.floor(xpos).astype(I32), 0, W - 2)
            fracs.append(xpos - lowest.astype(F32))
            hot[:, pl.ds(512 * g + 128 * s, 128)] = jnp.where(cells == lowest, 1.0, 0.0).astype(BF16)

    for copy in edge[:4] + sides:
        copy.wait()
    inside = jnp.where(iota((8, W), 0) < 4, jnp.where(lat < 3, 1, 0), jnp.where(lat > 0, 1, 0))
    for k in range(LEVELS):
        wf[k, pl.ds(H, 8), wide] = jnp.where(inside > 0, wi[k, pl.ds(H, 8)].astype(F32), 0.0)
    lane8 = iota((8, 128), 1)
    side = []
    for t in range(4):
        body = jnp.where(lane64 % 6 < 3, from_w[t], from_e[t])
        upper = jnp.where(lane8 % 6 < 3, from_nw[t], from_ne[t])
        lower = jnp.where(lane8 % 6 < 3, from_sw[t], from_se[t])
        side.append(jnp.concatenate([body, jnp.where(sub8[:, :128] < 4, upper, lower)], axis=0))

    def unpack(t, q, ref, at):
        values = pltpu.roll(side[t], (128 - 6 * q - 3) % 128, 1)
        if ref is wf:
            edge_rows = jnp.where(inside[:, :128] > 0, values[H:], 0.0)
            values = jnp.concatenate([values[:H], edge_rows], axis=0)
        return ref, at, values

    def unpack_all(blocks_of):
        held = []
        for t in blocks_of:
            for q, (ref, at) in planes_of(t):
                held.append(unpack(t, q, ref, at))
                if len(held) > 3:
                    ref, at, values = held.pop(0)
                    ref[at + (pl.ds(0, values.shape[0]), pl.ds(W, 128))] = values
        for ref, at, values in held:
            ref[at + (pl.ds(0, values.shape[0]), pl.ds(W, 128))] = values

    unpack_all((1, 2, 3))

    @pl.loop(0, LEVELS)
    def _(k):
        for strip in range(7):
            coefficients(k, strip, 384, EW)
        coefficients(k, 7, 0, EW)
        coefficients(k, 8, 0, EW)

    done = remote(got.at[pl.ds(1, 15)], got.at[pl.ds(1, 15)], p2_s, p2_r, east)
    done.wait_send()
    done.wait_recv()

    rims = {}

    def exchange(ref, number):
        def rim(a, b, i, peer):
            at = [ref.at[:, pl.ds(0, LEVELS), pl.ds(r, 1)] for r in (a, b)]
            return remote(at[0], at[1], row_s.at[2 * number + i], row_r.at[2 * number + i], peer)

        rims[number] = rim(H - 1, EH - 1, 0, north), rim(0, H, 1, south)
        for copy in rims[number]:
            copy.start()

    vals = got[...].reshape(128, 128)
    valsT = vals.T
    cols = (vals.astype(I32) - 1) & (W - 1)
    rowsT = (valsT.astype(I32) - 1) >> 9

    grown = [jnp.dot(part, spread[...], preferred_element_type=F32) for part in split(vals)]
    sub64 = iota((H, 128), 0)
    pick, hi_parts, lo_parts, ones = [], [], [], []
    for b, start in enumerate((0, PAY, 4 * PAY, 5 * PAY)):
        at = start + PAY - 1
        pick.append(jnp.where(sub64 == rowsT[at : at + 1], 1.0, 0.0))
        match = jnp.where(cols[:, at : at + 1] == targets[b // 2], 1.0, 0.0)
        hi_parts.append(match * grown[0][:, 128 * b : 128 * b + 128])
        lo_parts.append(match * grown[1][:, 128 * b : 128 * b + 128])
        ones.append(match)
    pick = jnp.concatenate(pick, axis=1).astype(BF16)
    onto = jnp.concatenate([jnp.concatenate(p, axis=0).astype(BF16) for p in (hi_parts, lo_parts, ones)], axis=1)
    beside = jnp.dot(pick, onto, preferred_element_type=F32)

    wide_lane = iota((128, W), 1)
    slots = (2 * PAY, 3 * PAY)
    own_rows = jnp.concatenate([rowsT[b + PAY - 1 : b + PAY] for b in slots], axis=1)
    own = jnp.where(iota((H, 256), 0) == own_rows, 1.0, 0.0)
    for c in range(20):
        value = jnp.concatenate([valsT[b + c : b + c + 1] for b in slots], axis=1)
        value_hi = value.astype(BF16).astype(F32)
        amat[pl.ds(H * c, H), pl.ds(0, 256)] = (own * value_hi).astype(BF16)
        amat[pl.ds(H * c, H), pl.ds(256, 256)] = (own * (value - value_hi)).astype(BF16)
    amat[pl.ds(H * 20, H), pl.ds(0, 256)] = own.astype(BF16)
    amat[pl.ds(H * 20, H), pl.ds(256, 256)] = jnp.zeros((H, 256), BF16)
    onto = [jnp.where(wide_lane == cols[:, b + PAY - 1 : b + PAY], 1.0, 0.0) for b in slots]
    onto = jnp.concatenate(onto + onto, axis=0).astype(BF16)
    added = jnp.dot(amat[...], onto, preferred_element_type=F32)
    keep = 1.0 - 0.5 * added[H * 20 :]
    for c in range(20):
        at = (c // LEVELS, c % LEVELS, pl.ds(0, H), wide)
        c0[at] = c0[at] * keep + added[H * c : H * c + H]
    body = side[0][:H]
    side[0] = body * (1.0 - 0.5 * beside[:, 256:384]) + beside[:, 0:128] + beside[:, 128:256]

    unpack_all((0,))
    exchange(c0, 0)

    tiles = EW // 128
    first_lane, last_lane = iota((8, 128), 1) == 0, iota((8, 128), 1) == 127
    first_row, last_row = iota((8, 128), 0) == 0, iota((8, 128), 0) == 7

    def sweep(src, dst, last, starts):
        @pl.loop(0, LEVELS)
        def _(k):
            def load(ref, at, i):
                return [ref[at + (pl.ds(8 * (i % STRIPS), 8), pl.ds(128 * j, 128))] for j in range(tiles)]

            started, fluxes, turned, below = {}, {}, {}, {}

            def start(i, n):
                here = load(src, (n, k), i)
                started[i, n] = here, [pltpu.roll(x, 127, 1) for x in here]

            def face(i, n):
                here, moved = started.pop((i, n))
                east_of = [jnp.where(last_lane, moved[(j + 1) % tiles], moved[j]) for j in range(tiles)]
                flux = [
                    a * x - b * y for a, b, x, y in zip(load(dx, (0, k), i), load(vx, (0, k), i), east_of, here)
                ]
                fluxes[i, n] = here, flux, [pltpu.roll(x, 1, 1) for x in flux]

            def north_flux(i, here, above):
                return [a * x - b * y for a, b, x, y in zip(load(dx, (1, k), i), load(vx, (1, k), i), above, here)]

            def finish(i, n):
                here, flux, moved = fluxes.pop((i, n))
                lifted = [pltpu.roll(x, 7, 0) for x in load(src, (n, k), i + 1)]
                above = [jnp.where(last_row, a, b) for a, b in zip(lifted, turned[i, n])]
                flux_n = north_flux(i, here, above)
                dropped = [pltpu.roll(x, 1, 0) for x in flux_n]
                higher = load(src, (n, k + 1), i)
                flux_v = [c * (x - y) for c, x, y in zip(load(dx, (2, k), i), higher, here)]
                flux_u = load(vbuf, (n,), i)
                rows = pl.ds(8 * i, 8)
                for j in range(tiles):
                    if last and j == tiles - 1:
                        continue
                    vbuf[n, rows, pl.ds(128 * j, 128)] = flux_v[j]
                    new = here[j] + (flux_n[j] - jnp.where(first_row, below[i, n][j], dropped[j]))
                    new = new + (flux[j] - jnp.where(first_lane, moved[j - 1], moved[j])) + (flux_v[j] - flux_u[j])
                    dst[n, k, rows, pl.ds(128 * j, 128)] = new
                turned[i + 1, n], below[i + 1, n] = lifted, dropped

            chunks = []
            for first, count in starts:
                for n in range(2):
                    prev = (first - 1) % STRIPS
                    tail, head = load(src, (n, k), prev), load(src, (n, k), first)
                    turned[first, n] = [pltpu.roll(x, 7, 0) for x in head]
                    above = [jnp.where(last_row, a, pltpu.roll(b, 7, 0)) for a, b in zip(turned[first, n], tail)]
                    below[first, n] = [pltpu.roll(x, 1, 0) for x in north_flux(prev, tail, above)]
                chunks += [(first + i, n) for i in range(count) for n in range(2)]
            for at in range(len(chunks) + 2 * GAP):
                for stage, work in enumerate((start, face, finish)):
                    if 0 <= at - stage * GAP < len(chunks):
                        work(*chunks[at - stage * GAP])

    for number, (src, dst) in enumerate(((c0, c1), (c1, c0), (c0, out_ref))):
        vbuf[:, pl.ds(0, H)] = jnp.zeros((2, H, EW), F32)
        sweep(src, dst, number == 2, [(1, 6)])
        for copy in rims[number]:
            copy.wait()
        sweep(src, dst, number == 2, [(7, 1), (0, 1)])
        if number < 2:
            exchange(dst, number + 1)

    plane = jnp.concatenate([out_ref[0, 0], out_ref[1, 0]], axis=0)
    nexts = pltpu.roll(plane, W - 1, 1)
    lhs = jnp.concatenate(list(split(plane)) + list(split(nexts)), axis=0)
    line = iota((H, 128), 0).astype(F32)
    for g in range(5):
        res = jnp.dot(lhs, hot[:, pl.ds(512 * g, 512)], preferred_element_type=F32)
        for s in range(4):
            part = res[:, 128 * s : 128 * s + 128]
            frac = fracs[4 * g + s]
            along = (1.0 - frac) * (part[0:128] + part[128:256]) + frac * (part[256:384] + part[384:512])
            ypos = blocks[g][s : s + 1, 384:512] * (H - 1.0)
            tent = jnp.maximum(0.0, 1.0 - jnp.abs(ypos - line))
            flag = blocks[g][s : s + 1, 512:640]
            for n in range(2):
                sample = jnp.sum(along[H * n : H * n + H] * tent, axis=0, keepdims=True)
                value = flag * (0.5 * blocks[g][s : s + 1, 128 * n : 128 * n + 128] + 0.5 * sample)
                if g in reach:
                    value = reach[g] * value
                fout_ref[4 * g + s, pl.ds(n, 1), :] = value


def shards(tracers, diffusivity, velocity, wet_mask, argo_rows, argo_dest, argo_cols, argo_count, float_values, float_pos, float_dest):
    vmem = pl.BlockSpec(memory_space=pltpu.VMEM)
    hbm = pl.BlockSpec(memory_space=pltpu.HBM)
    dma, scratch = pltpu.SemaphoreType.DMA, pltpu.VMEM
    return pl.pallas_call(
        kernel,
        out_shape=(
            pltpu.VMEM(tracers.shape, F32),
            pltpu.VMEM((20, 2, 128), F32),
        ),
        in_specs=[hbm] * 11,
        out_specs=(vmem, vmem),
        scratch_shapes=[
            scratch((2, LEVELS + 1, EH, EW), F32),
            scratch((2, LEVELS + 1, EH, EW), F32),
            scratch((3, LEVELS, EH, EW), F32),
            scratch((2, LEVELS, EH, EW), F32),
            scratch((LEVELS, EH, W), I32),
            scratch((LEVELS + 1, EH, EW), F32),
            scratch((2, EH, EW), F32),
            scratch((4, H, 128), F32),
            scratch((4, H, 128), F32),
            scratch((4, H, 128), F32),
            scratch((4, 8, 128), F32),
            scratch((4, 8, 128), F32),
            scratch((4, 8, 128), F32),
            scratch((4, 8, 128), F32),
            scratch((8, 4, 4, 1, 128), F32),
            scratch((8, 4, 4, 1, 128), F32),
            scratch((16, 8, 1, 128), F32),
            scratch((5, 8, 640), F32),
            scratch((4, 8, 640), F32),
            scratch((H * 21, 512), BF16),
            scratch((W, 2560), BF16),
            scratch((128, 512), BF16),
            scratch((128, 128), F32),
            scratch((1, 128), I32),
            scratch((1, 128), I32),
            pltpu.SMEM((1,), I32),
            scratch((16, 2, 128), F32),
            scratch((16, 2, 128), F32),
            scratch((1, 16), I32),
            dma((7,)), dma((12,)), dma, dma, dma, dma, dma((4,)), dma((4,)), dma((6,)), dma((6,)), dma((4,)), dma((4,)),
            dma((6,)), dma((6,)),
        ],
        compiler_params=pltpu.CompilerParams(
            collective_id=1, has_side_effects=True, vmem_limit_bytes=61 * 1024 * 1024
        ),
    )(
        tracers, diffusivity, velocity, wet_mask, argo_rows, argo_dest.reshape(1, -1), argo_cols.reshape(1, -1),
        argo_count, float_values, float_pos, float_dest.reshape(1, -1),
    )


def solution(mesh):
    grid4, grid3 = P(None, None, "lat", "lon"), P(None, "lat", "lon")
    tiles = ("lon", "lat")
    return jax.shard_map(
        shards,
        mesh=mesh,
        in_specs=(
            grid4, grid4, grid4, grid3, P(tiles, None), P(tiles, None), P(tiles), P(tiles),
            P(tiles, None, None), P(tiles, None, None), P(tiles, None),
        ),
        out_specs=(grid4, P(tiles, None, None)),
        check_vma=False,
    )
```
